32 devices in a mesh: row: 8 (over z, x), col: 4 (over y, core).
Axes of the slice: x: 2, y: 2, z: 4, core: 2. Of those that a mesh axis runs over, the one named last changes fastest.
Arguments:
- right_sides: float32 [4, 32, 128, 128], P(None, 'row'), may hold values from -6 to 6
- inverse_diag: float32 [4, 32, 128, 128], P(None, 'row', 'col'), may hold values from -1 to 2
- lower_blocks: float32 [3, 32, 16, 128, 128], P(None, 'row', None, 'col'), may hold values from -0.09375 to 0.09375
- depends_on: int32 [3, 32, 16], replicated, may hold values from 0 to 31, as said below
Outputs:
- solution: float32 [4, 32, 128, 128], P(None, 'row', 'col')
The draws below stay inside these ranges and needn't reach their ends.
Inputs may be any that keep to these rules, and one draw needn't show every extreme that they name: `depends_on`: in each level, the supernodes of one device along row name the supernodes of any one device along row at most 16 times in all, and some pair of devices reaches 16 in every level.
All inputs are finite; a program needn't handle non-finite values.
Results may differ from the reference program's by a relative error of at most 0.0001.
Values sent between devices are 32-bit elements; how exact they have to be, the bound alone decides.
No kernel may reach another device: no remote copies, remote signals or barrier semaphores. Data moves between devices by JAX's collectives and lax.ppermute only.
A program may use at most 64 MiB of HBM per device.

```python
import math
import jax
import jax.numpy as jnp
from jax import lax

S = 128
NRHS = 128
NB_DEV = 4
DEPS = 16
LEVELS = 4
NB = 32
CAP = 16


def draw_inverse_diag(key, part):
    first_key, second_key = jax.random.split(jax.random.fold_in(key, 11))
    noise = jnp.clip(jax.random.normal(first_key, (LEVELS, NB, S, S), jnp.float32), -5.0, 5.0) * (0.7 / math.sqrt(S))
    diagonal = jax.random.uniform(second_key, (LEVELS, NB, S), jnp.float32, 0.5, 1.5)
    identity = jnp.eye(S, dtype=jnp.float32)
    return jnp.tril(noise, -1) + diagonal[..., None] * identity


def draw_depends_on(key, part):
    entries = NB_DEV * DEPS
    devices = NB // NB_DEV
    tickets = devices * CAP

    def receiver(receiver_key):
        key_one, key_two, key_three, key_four = jax.random.split(receiver_key, 4)
        order = jax.random.permutation(key_one, tickets)
        focal = jax.random.randint(key_two, (), 0, devices)
        score = jnp.where(order // CAP == focal, 0, tickets) + jnp.arange(tickets)
        ranked = order[jnp.argsort(score)]
        chosen = ranked[:entries]
        chosen = chosen[jax.random.permutation(key_three, entries)]
        local_pick = jax.random.randint(key_four, (entries,), 0, NB_DEV)
        return chosen // CAP * NB_DEV + local_pick

    def one_level(level_key):
        return jax.vmap(receiver)(jax.random.split(level_key, devices)).reshape(NB, DEPS)
    level_keys = jax.random.split(jax.random.fold_in(key, 7), LEVELS - 1)
    return jax.vmap(one_level)(level_keys).astype(jnp.int32)


def steps_of(rng, extent, pieces, least, top_value):
    gain, own = 1.0, jax.random.fold_in(rng, 6)
    for position, parts in pieces:
        heights = jnp.exp(jax.random.uniform(jax.random.fold_in(own, position), (parts,), jnp.float32, least / len(pieces), top_value / len(pieces)))
        gain = gain * jnp.repeat(heights, extent[position] // parts).reshape([-1 if axis == position else 1 for axis in range(len(extent))])
    return gain


def centred(key, extent, spread, limit, cuts=(), kind=jnp.bfloat16):
    array = spread * jax.random.normal(key, extent, jnp.float32)
    if cuts:
        array = array * steps_of(key, extent, cuts, -0.22, 0.18)
    return jnp.clip(array, -limit, limit).astype(kind)


def setup_inputs(seed: int = 0) -> dict:
    keys = jax.random.split(jax.random.key(seed), 5)
    right_sides = centred(keys[0], (LEVELS, NB, S, NRHS), 1.0, 6.0, ((1, 8),), jnp.float32)
    inverse_diag = draw_inverse_diag(jax.random.fold_in(keys[4], 71), 0)
    lower_blocks = centred(keys[2], (LEVELS - 1, NB, DEPS, S, S), (2 * DEPS * S) ** -0.5, 0.09375, ((1, 8), (3, 4)), jnp.float32)
    depends_on = draw_depends_on(jax.random.fold_in(keys[4], 71), 0)
    return {"right_sides": right_sides, "inverse_diag": inverse_diag, "lower_blocks": lower_blocks, "depends_on": depends_on}


def reference(right_sides, inverse_diag, lower_blocks, depends_on):
    exact_mode = lax.Precision.HIGHEST
    current = jnp.einsum("jab,jbk->jak", inverse_diag[0], right_sides[0], precision=exact_mode)
    forward = [current]
    for level_no in range(1, LEVELS):
        picked = jnp.take(current, depends_on[level_no - 1], axis=0)
        update = jnp.einsum("jdba,jdbk->jak", lower_blocks[level_no - 1], picked, precision=exact_mode)
        current = jnp.einsum("jab,jbk->jak", inverse_diag[level_no], right_sides[level_no] - update, precision=exact_mode)
        forward.append(current)
    upper_sol = jnp.einsum("jab,jak->jbk", inverse_diag[LEVELS - 1], forward[LEVELS - 1], precision=exact_mode)
    solved = [upper_sol]
    for level_no in range(LEVELS - 2, -1, -1):
        contrib = jnp.einsum("jdba,jak->jdbk", lower_blocks[level_no], upper_sol, precision=exact_mode)
        returned = jax.ops.segment_sum(contrib.reshape(NB * DEPS, S, NRHS), depends_on[level_no].reshape(NB * DEPS), num_segments=NB)
        upper_sol = jnp.einsum("jab,jak->jbk", inverse_diag[level_no], forward[level_no] - returned, precision=exact_mode)
        solved.insert(0, upper_sol)
    return jnp.stack(solved)
```

```python
import functools

import jax
import jax.numpy as jnp
from jax import lax
from jax.experimental import pallas as pl
from jax.experimental.pallas import tpu as pltpu
from jax.sharding import PartitionSpec as P

F32 = jnp.float32
BF16 = jnp.bfloat16
EXACT = lax.Precision.HIGHEST
VMEM = pl.BlockSpec(memory_space=pltpu.VMEM)
SMEM = pl.BlockSpec(memory_space=pltpu.SMEM)
ANY = pl.BlockSpec(memory_space=pl.ANY)


def nn(a, b):
    return lax.dot_general(a, b, (((1,), (0,)), ((), ())), precision=EXACT, preferred_element_type=F32)


def nt(a, b):
    return lax.dot_general(a, b, (((1,), (1,)), ((), ())), precision=EXACT, preferred_element_type=F32)


def tn(a, b):
    return lax.dot_general(a, b, (((0,), (0,)), ((), ())), precision=EXACT, preferred_element_type=F32)


def half(a, b, contract):
    return lax.dot_general(a, b, ((contract[:1], contract[1:]), ((), ())), preferred_element_type=F32)


def split(value):
    high = value.astype(BF16)
    return high, (value - high.astype(F32)).astype(BF16)


def call(body, out_shape, in_specs, scratch=(), flops=0, moved=0, limit=40):
    return pl.pallas_call(
        body,
        out_shape=out_shape,
        in_specs=in_specs,
        out_specs=jax.tree.map(lambda _: VMEM, out_shape),
        scratch_shapes=list(scratch),
        compiler_params=pltpu.CompilerParams(vmem_limit_bytes=limit * 1024 * 1024),
        cost_estimate=pl.CostEstimate(flops=flops, bytes_accessed=moved, transcendentals=0),
    )


def swap(value, axis, mask):
    size = lax.axis_size(axis)
    return lax.ppermute(value, axis, [(i, i ^ mask) for i in range(size)])


def far_masks(size):
    masks, mask = [], size // 2
    while mask >= 4:
        masks.append(mask)
        mask //= 2
    return masks


def slot_of(mask, size):
    place = (mask & 3) * (size // 4)
    for step, far in enumerate(far_masks(size)):
        place = place + jnp.where((mask & far) != 0, 1 << step, 0)
    return place


def gather_row(own):
    held = own
    for mask in far_masks(lax.axis_size("row")):
        held = jnp.concatenate([held, swap(held, "row", mask)], axis=0)
    return [held] + [swap(held, "row", mask) for mask in (1, 2, 3)]


def scatter_row(parts):
    total = parts[0]
    got = [swap(part, "row", mask) for mask, part in zip((1, 2, 3), parts[1:])]
    total = total + got[0] + got[1] + got[2]
    other = None
    for mask in reversed(far_masks(lax.axis_size("row"))):
        if other is not None:
            total = total + other
        keep, send = jnp.split(total, 2, axis=0)
        total, other = keep, swap(send, "row", mask)
    return total, other


def first_kernel(inverse_ref, sides_ref, out_ref):
    for j in range(out_ref.shape[0]):
        out_ref[j] = nn(inverse_ref[j], sides_ref[j])


def turn_kernel(col_ref, sides_ref, out_ref, whole):
    count = out_ref.shape[1]
    start = pl.multiple_of(col_ref[0] * count, count)
    for i in range(out_ref.shape[0]):
        whole[i % 2] = sides_ref[i].T
        out_ref[i] = whole[i % 2, pl.ds(start, count), :]


def join_kernel(col_ref, *refs):
    parts, (high_ref, low_ref) = refs[:-2], refs[-2:]
    share = parts[0].shape[2]
    width = share * len(parts)
    for mask, part in enumerate(parts):
        offset = pl.multiple_of((col_ref[0] ^ mask) * share, share)
        for d in range(part.shape[1]):
            high, low = split(part[0, d])
            high_ref[0, pl.ds(d * width + offset, share), :] = high
            low_ref[0, pl.ds(d * width + offset, share), :] = low


def join_inverse_kernel(col_ref, *refs):
    parts, out_ref = refs[:-1], refs[-1]
    share = parts[0].shape[1]
    for mask, part in enumerate(parts):
        offset = pl.multiple_of((col_ref[0] ^ mask) * share, share)
        for i in range(part.shape[0]):
            out_ref[i, pl.ds(offset, share), :] = part[i]


def partial_kernel(col_ref, slot_ref, x0, x1, x2, x3, lower_ref, *refs):
    outs, (blocks, picked, turned) = refs[:-3], refs[-3:]
    count, fan_in, share, width = lower_ref.shape
    each = x0.shape[0]
    for q, x in enumerate((x0, x1, x2, x3)):
        blocks[q * each:(q + 1) * each] = x[...]
    for j in range(count):
        for d in range(fan_in):
            picked[j % 2, d * share:(d + 1) * share, :] = blocks[slot_ref[j * fan_in + d]]
        turned[j] = tn(picked[j % 2], lower_ref[j].reshape(fan_in * share, width))
    columns = outs[0].shape[1]
    for mask, out in enumerate(outs):
        start = pl.multiple_of((col_ref[0] ^ mask) * columns, columns)
        for j in range(count):
            out[j] = turned[j, pl.ds(start, columns), :]


def solve_first_kernel(u0, u1, u2, u3, sides_ref, inverse_ref, out_ref):
    for j in range(out_ref.shape[0]):
        rest = sides_ref[j] - ((u0[j] + u1[j]) + (u2[j] + u3[j]))
        out_ref[j] = nt(rest, inverse_ref[j])


def fetch(pairs, sems):
    copies = []
    for i in range(pairs[0][0].shape[0]):
        group = []
        for k, (source, target) in enumerate(pairs):
            copy = pltpu.make_async_copy(source.at[i], target.at[i], sems.at[i, k])
            copy.start()
            group.append(copy)
        copies.append(group)
    return copies


def forward_levels(slot_ref, xs, sides_ref, inverse_ref, high, low, copies, out_ref, blocks, picked):
    count, columns = out_ref.shape[:2]
    fan_in = slot_ref.shape[0] // count
    each = xs[0].shape[0]
    width = out_ref.shape[2]
    for q, x in enumerate(xs):
        for i in range(each):
            top, bottom = split(x[i])
            blocks[q * each + i, :columns] = top
            blocks[q * each + i, columns:] = bottom
    for j in range(count):
        for d in range(fan_in):
            picked[j, :, d * width:(d + 1) * width] = blocks[slot_ref[j * fan_in + d]]
    for j in range(count):
        for copy in copies[j]:
            copy.wait()
        both = half(picked[j], high[j], (1, 0)) + half(picked[j], low[j], (1, 0))
        update = both[:columns] + both[columns:]
        out_ref[j] = nt(sides_ref[j] - update, inverse_ref[j])


def backward_terms(slot_ref, solved, high, low, outs, total):
    count = high.shape[0]
    fan_in = slot_ref.shape[0] // count
    width = high.shape[2]
    total[...] = jnp.zeros_like(total)
    for j in range(count):
        value = solved(j)
        columns = value.shape[0]
        both = jnp.concatenate(split(value), axis=0)
        terms = half(both, high[j], (1, 1)) + half(both, low[j], (1, 1))
        terms = terms[:columns] + terms[columns:]
        for d in range(fan_in):
            slot = slot_ref[j * fan_in + d]
            total[slot] = total[slot] + terms[:, d * width:(d + 1) * width]
    each = outs[0].shape[0]
    for q, out in enumerate(outs):
        out[...] = total[q * each:(q + 1) * each]


def forward_kernel(slot_ref, x0, x1, x2, x3, sides_ref, inverse_ref, high_ref, low_ref, out_ref, high, low, sems, blocks, picked):
    copies = fetch(((high_ref, high), (low_ref, low)), sems)
    forward_levels(slot_ref, (x0, x1, x2, x3), sides_ref, inverse_ref, high, low, copies, out_ref, blocks, picked)


def top_kernel(
    slot_ref, x0, x1, x2, x3, sides_ref, inverse_ref, high_ref, low_ref, sol_ref, t0, t1, t2, t3,
    high, low, sems, blocks, picked, solved, total,
):
    copies = fetch(((high_ref, high), (low_ref, low)), sems)
    forward_levels(slot_ref, (x0, x1, x2, x3), sides_ref, inverse_ref, high, low, copies, solved, blocks, picked)

    def value(j):
        sol_ref[j] = nn(solved[j], inverse_ref[j])
        return sol_ref[j]

    backward_terms(slot_ref, value, high, low, (t0, t1, t2, t3), total)


def backward_kernel(
    slot_ref, ret0, ret1, forward_ref, inverse_ref, high_ref, low_ref, sol_ref, t0, t1, t2, t3, high, low, sems, total
):
    copies = fetch(((high_ref, high), (low_ref, low)), sems)

    def value(j):
        sol_ref[j] = nn(forward_ref[j] - (ret0[j] + ret1[j]), inverse_ref[j])
        for copy in copies[j]:
            copy.wait()
        return sol_ref[j]

    backward_terms(slot_ref, value, high, low, (t0, t1, t2, t3), total)


def last_kernel(col_ref, ret0, ret1, sides_ref, inverse_ref, s1, s2, s3, *refs):
    outs, (solved, packed) = refs[:-2], refs[-2:]
    count = sides_ref.shape[0]
    share = sides_ref.shape[2] // len(outs)
    for j in range(count):
        rest = nt(sides_ref[j], inverse_ref[j]) - (ret0[j] + ret1[j])
        solved[j] = nn(rest, inverse_ref[j])
    for level, source in enumerate((solved, s1, s2, s3)):
        for c in range(len(outs)):
            packed[c, level] = jnp.concatenate(
                [source[j, :, c * share:(c + 1) * share] for j in range(count)], axis=1
            )
    for mask, out in enumerate(outs):
        out[...] = packed[col_ref[0] ^ mask]


def out_kernel(col_ref, *refs):
    parts, (out_ref, whole) = refs[:-2], refs[-2:]
    levels, count, share, columns = out_ref.shape
    piece = parts[0].shape[1]
    for mask, part in enumerate(parts):
        start = pl.multiple_of((col_ref[0] ^ mask) * piece, piece)
        for level in range(levels):
            whole[level, pl.ds(start, piece), :] = part[level]
    for level in range(levels):
        out_ref[level] = whole[level].T.reshape(count, share, columns)


def collect(value):
    beside = swap(value, "col", 1)
    across = swap(value, "col", 2)
    return value, beside, across, swap(across, "col", 1)


def on_device(right_sides, inverse_diag, lower_blocks, depends_on):
    levels, count, width, columns = right_sides.shape
    share = inverse_diag.shape[2]
    fan_in = lower_blocks.shape[2]
    rows, cols = lax.axis_size("row"), lax.axis_size("col")
    my_row, my_col = lax.axis_index("row"), lax.axis_index("col")
    col = my_col.astype(jnp.int32).reshape(1)
    mine = columns // cols
    entries = count * fan_in
    wanted = lax.dynamic_slice_in_dim(depends_on, my_row * count, count, 1).reshape(levels - 1, entries)
    slots = slot_of((wanted // count) ^ my_row, rows) * count + wanted % count
    slots = [slots[i] for i in range(levels - 1)]

    def like(*shape, dtype=F32):
        return jax.ShapeDtypeStruct(shape, dtype)

    block = like(count, mine, width)
    quarter = like(rows // 4 * count, mine, width)
    solve_flops = 2 * count * mine * width * width * 6
    level_flops = 2 * entries * mine * width * width * 6
    level_bytes = 4 * entries * width * width

    first = call(
        first_kernel, like(count, share, columns), [VMEM] * 2, flops=solve_flops, moved=4 * count * width * width
    )(inverse_diag[0], right_sides[0])

    parts_inverse = collect(inverse_diag.reshape(levels * count, share, width))
    parts_lower = [None] * (levels - 1)
    for level in (1, 2, 0):
        parts_lower[level] = collect(lower_blocks[level])

    gathered = gather_row(first)

    sides = call(
        turn_kernel, like(levels * count, mine, width), [SMEM, VMEM],
        scratch=[pltpu.VMEM((2, columns, width), F32)], flops=0, moved=5 * levels * count * width * columns,
    )(col, right_sides.reshape(levels * count, width, columns))
    sides = [sides[i * count:(i + 1) * count] for i in range(levels)]

    partials = call(
        partial_kernel, [like(count, mine, width)] * cols, [SMEM, SMEM] + [VMEM] * 5,
        scratch=[
            pltpu.VMEM((rows * count, share, columns), F32),
            pltpu.VMEM((2, fan_in * share, columns), F32),
            pltpu.VMEM((count, columns, width), F32),
        ],
        flops=level_flops, moved=level_bytes // cols,
    )(col, slots[0], *gathered, lower_blocks[0])
    updates = [partials[0]] + [swap(partials[mask], "col", mask) for mask in range(1, cols)]

    inverse = call(
        join_inverse_kernel, like(levels * count, width, width), [SMEM] + [VMEM] * cols,
        flops=0, moved=8 * levels * count * width * width,
    )(col, *parts_inverse)
    inverse = [inverse[i * count:(i + 1) * count] for i in range(levels)]

    def join(parts):
        part_spec = pl.BlockSpec((1, fan_in, share, width), lambda j: (j, 0, 0, 0))
        out_spec = pl.BlockSpec((1, fan_in * width, width), lambda j: (j, 0, 0))
        return pl.pallas_call(
            join_kernel,
            grid=(count,),
            out_shape=[like(count, fan_in * width, width, dtype=BF16)] * 2,
            in_specs=[SMEM] + [part_spec] * cols,
            out_specs=[out_spec] * 2,
            compiler_params=pltpu.CompilerParams(vmem_limit_bytes=40 * 1024 * 1024),
            cost_estimate=pl.CostEstimate(flops=0, bytes_accessed=2 * level_bytes, transcendentals=0),
        )(col, *parts)

    lower = [None] * (levels - 1)
    for level in (1, 2, 0):
        lower[level] = join(parts_lower[level])

    fetched = [
        pltpu.VMEM((count, fan_in * width, width), BF16),
        pltpu.VMEM((count, fan_in * width, width), BF16),
        pltpu.SemaphoreType.DMA((count, 2)),
    ]
    picking = [
        pltpu.VMEM((rows * count, 2 * mine, width), BF16),
        pltpu.VMEM((count, 2 * mine, fan_in * width), BF16),
    ]
    total = [pltpu.VMEM((rows * count, mine, width), F32)]

    forward = [None] * levels
    forward[1] = call(
        solve_first_kernel, block, [VMEM] * 6, flops=solve_flops, moved=4 * count * width * width
    )(*updates, sides[1], inverse[1])
    for level in range(2, levels - 1):
        forward[level] = call(
            forward_kernel, block, [SMEM] + [VMEM] * 6 + [ANY] * 2, scratch=fetched + picking,
            flops=level_flops, moved=level_bytes,
        )(slots[level - 1], *gather_row(forward[level - 1]), sides[level], inverse[level], *lower[level - 1])

    solved = [None] * levels
    top = levels - 1
    solved[top], *terms = call(
        top_kernel, [block] + [quarter] * 4, [SMEM] + [VMEM] * 6 + [ANY] * 2,
        scratch=fetched + picking + [pltpu.VMEM((count, mine, width), F32)] + total,
        flops=2 * level_flops, moved=level_bytes,
    )(slots[top - 1], *gather_row(forward[top - 1]), sides[top], inverse[top], *lower[top - 1])
    for level in range(top - 1, 0, -1):
        solved[level], *terms = call(
            backward_kernel, [block] + [quarter] * 4, [SMEM] + [VMEM] * 4 + [ANY] * 2,
            scratch=fetched + total, flops=level_flops, moved=level_bytes,
        )(slots[level - 1], *scatter_row(terms), forward[level], inverse[level], *lower[level - 1])

    pieces = call(
        last_kernel, [like(levels, mine, count * share)] * cols, [SMEM] + [VMEM] * (4 + top),
        scratch=[
            pltpu.VMEM((count, mine, width), F32),
            pltpu.VMEM((cols, levels, mine, count * share), F32),
        ],
        flops=2 * solve_flops, moved=8 * count * width * width,
    )(col, *scatter_row(terms), sides[0], inverse[0], *solved[1:])
    pieces = [pieces[0]] + [swap(pieces[mask], "col", mask) for mask in range(1, cols)]
    return call(
        out_kernel, like(levels, count, share, columns), [SMEM] + [VMEM] * cols,
        scratch=[pltpu.VMEM((levels, columns, count * share), F32)],
        flops=0, moved=8 * levels * count * share * columns,
    )(col, *pieces)


def solution(mesh):
    return jax.shard_map(
        on_device,
        mesh=mesh,
        in_specs=(
            P(None, "row", None, None),
            P(None, "row", "col", None),
            P(None, "row", None, "col", None),
            P(),
        ),
        out_specs=P(None, "row", "col", None),
        check_vma=False,
    )
```

```python
import functools

import jax
import jax.numpy as jnp
from jax import lax
from jax.experimental import pallas as pl
from jax.experimental.pallas import tpu as pltpu
from jax.sharding import PartitionSpec as P

F32 = jnp.float32
BF16 = jnp.bfloat16
EXACT = lax.Precision.HIGHEST
VMEM = pl.BlockSpec(memory_space=pltpu.VMEM)
SMEM = pl.BlockSpec(memory_space=pltpu.SMEM)
ANY = pl.BlockSpec(memory_space=pl.ANY)
HBM = pl.BlockSpec(memory_space=pltpu.HBM)
TINY = pl.CostEstimate(flops=1, bytes_accessed=1, transcendentals=0)


def nn(a, b):
    return lax.dot_general(a, b, (((1,), (0,)), ((), ())), precision=EXACT, preferred_element_type=F32)


def half(a, b, contract):
    return lax.dot_general(a, b, ((contract[:1], contract[1:]), ((), ())), preferred_element_type=F32)


def split(value):
    high = value.astype(BF16)
    return high, (value - high.astype(F32)).astype(BF16)


def times(value, pair):
    rows, width = value.shape[0], pair.shape[1] // 2
    both = half(jnp.concatenate(split(value), axis=0), pair, (1, 0))
    both = both[:, :width] + both[:, width:]
    return both[:rows] + both[rows:]


def times_turned(value, pair):
    rows = value.shape[0]
    high, low = split(value)
    wide = jnp.concatenate([jnp.concatenate([high, high], axis=1), jnp.concatenate([low, low], axis=1)], axis=0)
    both = half(wide, pair, (1, 1))
    return both[:rows] + both[rows:]


def call(body, out_shape, in_specs, scratch=(), limit=24):
    return pl.pallas_call(
        body,
        out_shape=out_shape,
        in_specs=in_specs,
        out_specs=jax.tree.map(lambda _: VMEM, out_shape),
        scratch_shapes=list(scratch),
        compiler_params=pltpu.CompilerParams(vmem_limit_bytes=limit * 1024 * 1024),
        cost_estimate=TINY,
    )


def swap(value, axis, mask):
    size = lax.axis_size(axis)
    return lax.ppermute(value, axis, [(i, i ^ mask) for i in range(size)])


def far_masks(size):
    masks, mask = [], size // 2
    while mask >= 4:
        masks.append(mask)
        mask //= 2
    return masks


def slot_of(mask, size):
    place = (mask & 3) * (size // 4)
    for step, far in enumerate(far_masks(size)):
        place = place + jnp.where((mask & far) != 0, 1 << step, 0)
    return place


def gather_row(own):
    held = own
    for mask in far_masks(lax.axis_size("row")):
        got = swap(held, "row", mask)
        held = jnp.concatenate([held, got], axis=0)
    return got, [held] + [swap(held, "row", mask) for mask in (1, 2, 3)]


def scatter_row(parts):
    total = parts[0]
    got = [swap(part, "row", mask) for mask, part in zip((1, 2, 3), parts[1:])]
    total = total + got[0] + got[1] + got[2]
    other = None
    for mask in reversed(far_masks(lax.axis_size("row"))):
        if other is not None:
            total = total + other
        keep, send = jnp.split(total, 2, axis=0)
        total, other = keep, swap(send, "row", mask)
    return total, other


def first_kernel(level, inverse_ref, sides_ref, lower_ref, out_ref, early_ref, inverse, sides, sems):
    copies = [
        pltpu.make_async_copy(inverse_ref.at[0], inverse, sems.at[0]),
        pltpu.make_async_copy(sides_ref.at[0], sides, sems.at[1]),
        pltpu.make_async_copy(lower_ref.at[level, pl.ds(0, early_ref.shape[0])], early_ref, sems.at[2]),
    ]
    for copy in copies:
        copy.start()
    for copy in copies[:2]:
        copy.wait()
    for j in range(out_ref.shape[0]):
        out_ref[j] = nn(inverse[j], sides[j])
    copies[2].wait()


def turn_kernel(col_ref, sides_ref, out_ref, whole):
    count = out_ref.shape[1]
    start = pl.multiple_of(col_ref[0] * count, count)
    for i in range(out_ref.shape[0]):
        whole[i % 2] = sides_ref[i].T
        out_ref[i] = whole[i % 2, pl.ds(start, count), :]


def join_kernel(col_ref, *refs):
    parts, out_ref = refs[:-1], refs[-1]
    share, width = parts[0].shape[2:]
    for mask, part in enumerate(parts):
        offset = pl.multiple_of((col_ref[0] ^ mask) * share, share)
        for d in range(part.shape[1]):
            high, low = split(part[0, d])
            out_ref[0, pl.ds(d * width + offset, share), :width] = high
            out_ref[0, pl.ds(d * width + offset, share), width:] = low


def join_inverse_kernel(col_ref, *refs):
    parts, (out_ref, token_ref) = refs[:-2], refs[-2:]
    token_ref[...] = jnp.zeros_like(token_ref)
    share, width = parts[0].shape[1:]
    for mask, part in enumerate(parts):
        offset = pl.multiple_of((col_ref[0] ^ mask) * share, share)
        for i in range(part.shape[0]):
            high, low = split(part[i])
            out_ref[i, pl.ds(offset, share), :width] = high
            out_ref[i, pl.ds(offset, share), width:] = low


def stand_kernel(lower_ref, out_ref, own, sem):
    count, fan_in, share, width = own.shape
    copy = pltpu.make_async_copy(lower_ref.at[0], own, sem)
    copy.start()
    copy.wait()
    for j in range(count):
        high, low = split(own[j].reshape(fan_in * share, width).T)
        out_ref[j, :width] = high
        out_ref[j, width:] = low


def partial_kernel(col_ref, slot_ref, x0, x1, x2, x3, lower_ref, early_ref, token_ref, *refs):
    outs, (blocks, picked, turned) = refs[:-3], refs[-3:]
    count = lower_ref.shape[0]
    fan_in = slot_ref.shape[0] // count
    each, share, columns = x0.shape
    width = lower_ref.shape[1] // 2
    for q, x in enumerate((x0, x1, x2, x3)):
        for i in range(each):
            high, low = split(x[i])
            blocks[q * each + i, :, :columns] = high
            blocks[q * each + i, :, columns:] = low
    for j in range(count):
        for d in range(fan_in):
            picked[j, d * share:(d + 1) * share, :] = blocks[slot_ref[j * fan_in + d]]
    for j in range(count):
        both = half(lower_ref[j], picked[j], (1, 0))
        both = both[:width] + both[width:]
        turned[j] = (both[:, :columns] + both[:, columns:]).T
    columns = outs[0].shape[1]
    for place, mask in enumerate((0, 2, 1, 3)):
        start = pl.multiple_of((col_ref[0] ^ mask) * columns, columns)
        out = outs[place] if place < 2 else outs[2].at[pl.ds((place - 2) * count, count)]
        for j in range(count):
            out[j] = turned[j, pl.ds(start, columns), :]


def solve_first_kernel(u0, u1, u2, sides_ref, inverse_ref, out_ref):
    for j in range(out_ref.shape[0]):
        out_ref[j] = times_turned(sides_ref[j] - ((u0[j] + u1[j]) + u2[j]), inverse_ref[j])


def block_of(lower, j):
    some = lower[0].shape[0]
    return lower[j // some][j % some]


def forward_levels(slot_ref, xs, sides_ref, inverse_ref, lower, out_ref, blocks, picked):
    count, columns, width = out_ref.shape
    fan_in = slot_ref.shape[0] // count
    each = xs[0].shape[0]
    for q, x in enumerate(xs):
        for i in range(each):
            high, low = split(x[i])
            blocks[q * each + i, :columns] = high
            blocks[q * each + i, columns:] = low
    for j in range(count):
        for d in range(fan_in):
            picked[j, :, d * width:(d + 1) * width] = blocks[slot_ref[j * fan_in + d]]
    rest = []
    for j in range(count):
        both = half(picked[j], block_of(lower, j), (1, 0))
        both = both[:, :width] + both[:, width:]
        rest.append(sides_ref[j] - (both[:columns] + both[columns:]))
    for j in range(count):
        out_ref[j] = times_turned(rest[j], inverse_ref[j])


def backward_terms(slot_ref, solved, lower, outs, total):
    count, _, width = solved.shape
    fan_in = slot_ref.shape[0] // count
    total[...] = jnp.zeros_like(total)
    for j in range(count):
        terms = times_turned(solved[j], block_of(lower, j))
        for d in range(fan_in):
            slot = slot_ref[j * fan_in + d]
            total[slot] = total[slot] + terms[:, d * width:(d + 1) * width]
    each = outs[0].shape[0]
    for q, out in enumerate(outs):
        out[...] = total[q * each:(q + 1) * each]


def forward_kernel(chunks, slot_ref, x0, x1, x2, x3, sides_ref, inverse_ref, *refs):
    lower, (out_ref, blocks, picked) = refs[:chunks], refs[chunks:]
    forward_levels(slot_ref, (x0, x1, x2, x3), sides_ref, inverse_ref, lower, out_ref, blocks, picked)


def top_kernel(chunks, slot_ref, x0, x1, x2, x3, sides_ref, inverse_ref, *refs):
    lower, outs = refs[:chunks], refs[chunks + 1:chunks + 5]
    sol_ref, (blocks, picked, solved, total) = refs[chunks], refs[chunks + 5:]
    forward_levels(slot_ref, (x0, x1, x2, x3), sides_ref, inverse_ref, lower, solved, blocks, picked)
    for j in range(sol_ref.shape[0]):
        sol_ref[j] = times(solved[j], inverse_ref[j])
    backward_terms(slot_ref, sol_ref, lower, outs, total)


def backward_kernel(chunks, slot_ref, ret0, ret1, forward_ref, inverse_ref, *refs):
    lower, outs = refs[:chunks], refs[chunks + 1:chunks + 5]
    sol_ref, total = refs[chunks], refs[chunks + 5]
    for j in range(sol_ref.shape[0]):
        sol_ref[j] = times(forward_ref[j] - (ret0[j] + ret1[j]), inverse_ref[j])
    backward_terms(slot_ref, sol_ref, lower, outs, total)


def last_kernel(col_ref, ret0, ret1, sides_ref, inverse_ref, s1, s2, s3, *refs):
    outs, (solved, packed) = refs[:-2], refs[-2:]
    count = sides_ref.shape[0]
    share = sides_ref.shape[2] // len(outs)
    for j in range(count):
        rest = times_turned(sides_ref[j], inverse_ref[j]) - (ret0[j] + ret1[j])
        solved[j] = times(rest, inverse_ref[j])
    for level, source in enumerate((solved, s1, s2, s3)):
        for c in range(len(outs)):
            packed[c, level] = jnp.concatenate(
                [source[j, :, c * share:(c + 1) * share] for j in range(count)], axis=1
            )
    for mask, out in enumerate(outs):
        out[...] = packed[col_ref[0] ^ mask]


def out_kernel(col_ref, *refs):
    parts, (out_ref, whole) = refs[:-2], refs[-2:]
    levels, count, share, columns = out_ref.shape
    piece = parts[0].shape[1]
    for mask, part in enumerate(parts):
        start = pl.multiple_of((col_ref[0] ^ mask) * piece, piece)
        for level in range(levels):
            whole[level, pl.ds(start, piece), :] = part[level]
    for level in range(levels):
        out_ref[level] = whole[level].T.reshape(count, share, columns)


def same_kernel(value_ref, *refs):
    refs[-1][...] = value_ref[...]


def after(value, *others):
    return pl.pallas_call(
        same_kernel,
        out_shape=jax.ShapeDtypeStruct(value.shape, value.dtype),
        in_specs=[VMEM] * (1 + len(others)),
        out_specs=VMEM,
        compiler_params=pltpu.CompilerParams(vmem_limit_bytes=8 * 1024 * 1024),
        cost_estimate=TINY,
    )(value, *others)


def pack_kernel(level, start, lower_ref, *refs):
    out_ref, sem = refs[-2:]
    copy = pltpu.make_async_copy(lower_ref.at[level, pl.ds(start, out_ref.shape[0])], out_ref, sem)
    copy.start()
    copy.wait()


def pack(lower_blocks, level, start, size, *others):
    return pl.pallas_call(
        functools.partial(pack_kernel, level, start),
        out_shape=jax.ShapeDtypeStruct((size,) + lower_blocks.shape[2:], F32),
        in_specs=[HBM] + [VMEM] * len(others),
        out_specs=VMEM,
        scratch_shapes=[pltpu.SemaphoreType.DMA],
        compiler_params=pltpu.CompilerParams(vmem_limit_bytes=8 * 1024 * 1024),
        cost_estimate=TINY,
    )(lower_blocks, *others)


def on_device(right_sides, inverse_diag, lower_blocks, depends_on):
    levels, count, width, columns = right_sides.shape
    share = inverse_diag.shape[2]
    fan_in = lower_blocks.shape[2]
    rows, cols = lax.axis_size("row"), lax.axis_size("col")
    my_row, my_col = lax.axis_index("row"), lax.axis_index("col")
    col = my_col.astype(jnp.int32).reshape(1)
    mine = columns // cols
    entries = count * fan_in
    wanted = lax.dynamic_slice_in_dim(depends_on, my_row * count, count, 1).reshape(levels - 1, entries)
    slots = slot_of((wanted // count) ^ my_row, rows) * count + wanted % count
    slots = [slots[i] for i in range(levels - 1)]

    def like(*shape, dtype=F32):
        return jax.ShapeDtypeStruct(shape, dtype)

    block = like(count, mine, width)
    quarter = like(rows // 4 * count, mine, width)

    def join(level, start, across):
        some = across.shape[0]
        own_spec = pl.BlockSpec((None, 1, fan_in, share, width), lambda j: (level, start + j, 0, 0, 0))
        part_spec = pl.BlockSpec((1, fan_in, share, width), lambda j: (j, 0, 0, 0))
        out_spec = pl.BlockSpec((1, fan_in * width, 2 * width), lambda j: (j, 0, 0))
        return pl.pallas_call(
            join_kernel,
            grid=(some,),
            out_shape=like(some, fan_in * width, 2 * width, dtype=BF16),
            in_specs=[SMEM, own_spec, own_spec, part_spec, part_spec],
            out_specs=out_spec,
            compiler_params=pltpu.CompilerParams(vmem_limit_bytes=24 * 1024 * 1024),
            cost_estimate=TINY,
        )(col, lower_blocks, lower_beside, *near(across))

    def near(value):
        return value, swap(value, "col", 1)

    top = levels - 1
    middle = count // 2
    first, early = call(
        functools.partial(first_kernel, 1), [like(count, share, columns), like(middle, fan_in, share, width)], [HBM] * 3,
        scratch=[
            pltpu.VMEM((count, share, width), F32),
            pltpu.VMEM((count, width, columns), F32),
            pltpu.SemaphoreType.DMA((3,)),
        ],
        limit=60,
    )(inverse_diag, right_sides, lower_blocks)
    early = swap(early, "col", 2)
    _, gathered = gather_row(first)
    all_inverse = inverse_diag.reshape(levels * count, share, width)
    parts_inverse = near(all_inverse) + near(swap(all_inverse, "col", 2))
    lower_beside = swap(lower_blocks, "col", 1)

    inverse, token = call(
        join_inverse_kernel, [like(levels * count, width, 2 * width, dtype=BF16), like(8, width)], [SMEM] + [VMEM] * cols
    )(col, *parts_inverse)
    inverse = [inverse[i * count:(i + 1) * count] for i in range(levels)]

    sides = call(
        turn_kernel, like(levels * count, mine, width), [SMEM, VMEM],
        scratch=[pltpu.VMEM((2, columns, width), F32)],
    )(col, right_sides.reshape(levels * count, width, columns))
    sides = [sides[i * count:(i + 1) * count] for i in range(levels)]

    standing = call(
        stand_kernel, like(count, 2 * width, fan_in * share, dtype=BF16), [HBM],
        scratch=[pltpu.VMEM(lower_blocks.shape[1:], F32), pltpu.SemaphoreType.DMA],
    )(lower_blocks)
    kept, passed, sent = call(
        partial_kernel, [block] * 2 + [like(2 * count, mine, width)], [SMEM] * 2 + [VMEM] * 7,
        scratch=[
            pltpu.VMEM((rows * count, share, 2 * columns), BF16),
            pltpu.VMEM((count, fan_in * share, 2 * columns), BF16),
            pltpu.VMEM((count, columns, width), F32),
        ],
    )(col, slots[0], *gathered, standing, early, token)
    beside = swap(sent, "col", 1)
    across = swap(passed + beside[count:], "col", 2)

    late = swap(pack(lower_blocks, 1, middle, count - middle, across), "col", 2)

    picking = [
        pltpu.VMEM((rows * count, 2 * mine, width), BF16),
        pltpu.VMEM((count, 2 * mine, fan_in * width), BF16),
    ]
    total = [pltpu.VMEM((rows * count, mine, width), F32)]

    forward, lower = [None] * levels, [None] * (levels - 1)
    forward[1] = call(solve_first_kernel, block, [VMEM] * 5)(
        kept, beside[:count], across, sides[1], inverse[1]
    )

    got, gathered = gather_row(forward[1])
    whole_early = swap(pack(lower_blocks, 2, 0, middle, forward[1]), "col", 2)
    whole_late = swap(pack(lower_blocks, 2, middle, count - middle, got), "col", 2)
    lower[1] = [
        join(1, 0, early),
        join(1, middle, after(late, got)),
    ]
    forward[2] = call(
        functools.partial(forward_kernel, len(lower[1])), block, [SMEM] + [VMEM] * 6 + [VMEM] * len(lower[1]),
        scratch=picking,
    )(slots[1], *gathered, sides[2], inverse[2], *lower[1])

    last = swap(pack(lower_blocks, 0, 0, count, forward[2]), "col", 2)
    got, gathered = gather_row(forward[2])
    lower[2] = [
        join(2, 0, after(whole_early, got)),
        join(2, middle, after(whole_late, *gathered[1:])),
    ]

    solved = [None] * levels
    solved[top], *terms = call(
        functools.partial(top_kernel, len(lower[2])), [block] + [quarter] * 4,
        [SMEM] + [VMEM] * 6 + [VMEM] * len(lower[2]),
        scratch=picking + [pltpu.VMEM((count, mine, width), F32)] + total,
    )(slots[2], *gathered, sides[top], inverse[top], *lower[2])

    returned = scatter_row(terms)
    solved[2], *terms = call(
        functools.partial(backward_kernel, len(lower[1])), [block] + [quarter] * 4,
        [SMEM] + [VMEM] * 4 + [VMEM] * len(lower[1]), scratch=total,
    )(slots[1], *returned, forward[2], inverse[2], *lower[1])

    returned = scatter_row(terms)
    lower[0] = [join(0, 0, after(last, solved[2]))]
    solved[1], *terms = call(
        functools.partial(backward_kernel, len(lower[0])), [block] + [quarter] * 4,
        [SMEM] + [VMEM] * 4 + [VMEM] * len(lower[0]), scratch=total,
    )(slots[0], *returned, forward[1], inverse[1], *lower[0])

    pieces = call(
        last_kernel, [like(levels, mine, count * share)] * cols, [SMEM] + [VMEM] * (4 + top),
        scratch=[
            pltpu.VMEM((count, mine, width), F32),
            pltpu.VMEM((cols, levels, mine, count * share), F32),
        ],
    )(col, *scatter_row(terms), sides[0], inverse[0], *solved[1:])
    pieces = [pieces[0]] + [swap(pieces[mask], "col", mask) for mask in range(1, cols)]
    return call(
        out_kernel, like(levels, count, share, columns), [SMEM] + [VMEM] * cols,
        scratch=[pltpu.VMEM((levels, columns, count * share), F32)],
    )(col, *pieces)


def solution(mesh):
    return jax.shard_map(
        on_device,
        mesh=mesh,
        in_specs=(
            P(None, "row", None, None),
            P(None, "row", "col", None),
            P(None, "row", None, "col", None),
            P(),
        ),
        out_specs=P(None, "row", "col", None),
        check_vma=False,
    )
```

```python
import functools

import jax
import jax.numpy as jnp
from jax import lax
from jax.experimental import pallas as pl
from jax.experimental.pallas import tpu as pltpu
from jax.sharding import PartitionSpec as P

F32 = jnp.float32
BF16 = jnp.bfloat16
EXACT = lax.Precision.HIGHEST
VMEM = pl.BlockSpec(memory_space=pltpu.VMEM)
SMEM = pl.BlockSpec(memory_space=pltpu.SMEM)
ANY = pl.BlockSpec(memory_space=pl.ANY)
HBM = pl.BlockSpec(memory_space=pltpu.HBM)
TINY = pl.CostEstimate(flops=1, bytes_accessed=1, transcendentals=0)


def nn(a, b):
    return lax.dot_general(a, b, (((1,), (0,)), ((), ())), precision=EXACT, preferred_element_type=F32)


def half(a, b, contract):
    return lax.dot_general(a, b, ((contract[:1], contract[1:]), ((), ())), preferred_element_type=F32)


def split(value):
    high = value.astype(BF16)
    return high, (value - high.astype(F32)).astype(BF16)


def times(value, pair):
    rows, width = value.shape[0], pair.shape[1] // 2
    both = half(jnp.concatenate(split(value), axis=0), pair, (1, 0))
    both = both[:, :width] + both[:, width:]
    return both[:rows] + both[rows:]


def times_turned(value, pair):
    rows = value.shape[0]
    high, low = split(value)
    wide = jnp.concatenate([jnp.concatenate([high, high], axis=1), jnp.concatenate([low, low], axis=1)], axis=0)
    both = half(wide, pair, (1, 1))
    return both[:rows] + both[rows:]


def call(body, out_shape, in_specs, scratch=(), limit=24):
    return pl.pallas_call(
        body,
        out_shape=out_shape,
        in_specs=in_specs,
        out_specs=jax.tree.map(lambda _: VMEM, out_shape),
        scratch_shapes=list(scratch),
        compiler_params=pltpu.CompilerParams(vmem_limit_bytes=limit * 1024 * 1024),
        cost_estimate=TINY,
    )


def swap(value, axis, mask):
    size = lax.axis_size(axis)
    return lax.ppermute(value, axis, [(i, i ^ mask) for i in range(size)])


def far_masks(size):
    masks, mask = [], size // 2
    while mask >= 4:
        masks.append(mask)
        mask //= 2
    return masks


def slot_of(mask, size):
    place = (mask & 3) * (size // 4)
    for step, far in enumerate(far_masks(size)):
        place = place + jnp.where((mask & far) != 0, 1 << step, 0)
    return place


def gather_row(own):
    held, got = own, own
    for mask in far_masks(lax.axis_size("row")):
        got = swap(held, "row", mask)
        held = jnp.concatenate([held, got], axis=0)
    return got, [held] + [swap(held, "row", mask) for mask in (1, 2, 3)]


def scatter_row(parts):
    total = parts[0]
    got = [swap(part, "row", mask) for mask, part in zip((1, 2, 3), parts[1:])]
    total = total + got[0] + got[1] + got[2]
    other = None
    for mask in reversed(far_masks(lax.axis_size("row"))):
        if other is not None:
            total = total + other
        keep, send = jnp.split(total, 2, axis=0)
        total, other = keep, swap(send, "row", mask)
    return got, (total, other)


def first_kernel(level, inverse_ref, sides_ref, lower_ref, out_ref, early_ref, inverse, sides, sems):
    copies = [
        pltpu.make_async_copy(inverse_ref.at[0], inverse, sems.at[0]),
        pltpu.make_async_copy(sides_ref.at[0], sides, sems.at[1]),
        pltpu.make_async_copy(lower_ref.at[level - 1, pl.ds(0, early_ref.shape[0])], early_ref, sems.at[2]),
    ]
    for copy in copies:
        copy.start()
    for copy in copies[:2]:
        copy.wait()
    for j in range(out_ref.shape[0]):
        out_ref[j] = nn(inverse[j], sides[j])
    copies[2].wait()


def turn_kernel(col_ref, sides_ref, out_ref, whole):
    count = out_ref.shape[1]
    start = pl.multiple_of(col_ref[0] * count, count)
    for i in range(out_ref.shape[0]):
        whole[i % 2] = sides_ref[i].T
        out_ref[i] = whole[i % 2, pl.ds(start, count), :]


def join_kernel(col_ref, *refs):
    parts, out_ref = refs[:-1], refs[-1]
    share, width = parts[0].shape[2:]
    for mask, part in enumerate(parts):
        offset = pl.multiple_of((col_ref[0] ^ mask) * share, share)
        for d in range(part.shape[1]):
            high, low = split(part[0, d])
            out_ref[0, pl.ds(d * width + offset, share), :width] = high
            out_ref[0, pl.ds(d * width + offset, share), width:] = low


def join_inverse_kernel(col_ref, *refs):
    parts, (out_ref, token_ref) = refs[:-2], refs[-2:]
    token_ref[...] = jnp.zeros_like(token_ref)
    share, width = parts[0].shape[1:]
    for mask, part in enumerate(parts):
        offset = pl.multiple_of((col_ref[0] ^ mask) * share, share)
        for i in range(part.shape[0]):
            high, low = split(part[i])
            out_ref[i, pl.ds(offset, share), :width] = high
            out_ref[i, pl.ds(offset, share), width:] = low


def stand_kernel(level, lower_ref, after_ref, out_ref, own, sem):
    count, fan_in, share, width = own.shape
    copy = pltpu.make_async_copy(lower_ref.at[level], own, sem)
    copy.start()
    copy.wait()
    for j in range(count):
        high, low = split(own[j].reshape(fan_in * share, width).T)
        out_ref[j, :width] = high
        out_ref[j, width:] = low


def fold_kernel(lower_ref, own_inverse_ref, sides_ref, inverse_ref, out_ref, base_ref, own, own_inverse, sides, sems):
    count, fan_in, share, width = own.shape
    copies = [
        pltpu.make_async_copy(lower_ref.at[0], own, sems.at[0]),
        pltpu.make_async_copy(own_inverse_ref.at[1], own_inverse, sems.at[1]),
        pltpu.make_async_copy(sides_ref.at[1], sides, sems.at[2]),
    ]
    for copy in copies:
        copy.start()
    for copy in copies:
        copy.wait()
    for j in range(count):
        high, low = split(times_turned(own[j].reshape(fan_in * share, width), inverse_ref[j]).T)
        out_ref[j, :width] = high
        out_ref[j, width:] = low
        base_ref[j] = nn(own_inverse[j], sides[j])


def partial_kernel(turn, col_ref, slot_ref, x0, x1, x2, x3, lower_ref, *refs):
    outs, (blocks, picked, sums) = refs[-6:-3], refs[-3:]
    count = lower_ref.shape[0]
    fan_in = slot_ref.shape[0] // count
    each, share, columns = x0.shape
    width = lower_ref.shape[1] // 2
    for q, x in enumerate((x0, x1, x2, x3)):
        for i in range(each):
            high, low = split(x[i])
            blocks[q * each + i, :, :columns] = high
            blocks[q * each + i, :, columns:] = low
    for j in range(count):
        for d in range(fan_in):
            picked[j, d * share:(d + 1) * share, :] = blocks[slot_ref[j * fan_in + d]]
    for j in range(count):
        both = half(lower_ref[j], picked[j], (1, 0))
        both = both[:width] + both[width:]
        both = both[:, :columns] + both[:, columns:]
        sums[j] = both.T if turn else both
    each, piece, _ = outs[0].shape
    if turn:
        sums[count] = refs[0][...].reshape(count * share, columns).T
    for place, mask in enumerate((0, 2, 1, 3)):
        start = pl.multiple_of((col_ref[0] ^ mask) * piece, piece)
        out = outs[place] if place < 2 else outs[2].at[pl.ds((place - 2) * each, each)]
        for j in range(each):
            out[j] = sums[j, pl.ds(start, piece), :]


def solve_kernel(col_ref, u0, u1, u2, sides_ref, inverse_ref, out_ref, lower_ref, parts):
    count = out_ref.shape[0]
    share = u0.shape[2] // count
    for j in range(count):
        out_ref[j] = times_turned(sides_ref[j] - ((u0[j] + u1[j]) + u2[j]), inverse_ref[j])
    parts[0], parts[1], parts[2], parts[3] = u0[count], u1[count], u2[count], u2[count + 1]
    for c in range(parts.shape[0]):
        part = parts[col_ref[0] ^ c]
        for j in range(count):
            lower_ref[j, :, c * share:(c + 1) * share] = part[:, j * share:(j + 1) * share]


def block_of(lower, j):
    for some in lower:
        if j < some.shape[0]:
            return some[j]
        j -= some.shape[0]


def forward_levels(slot_ref, xs, sides_ref, inverse_ref, lower, out_ref, blocks, picked):
    count, columns, width = out_ref.shape
    fan_in = slot_ref.shape[0] // count
    each = xs[0].shape[0]
    for q, x in enumerate(xs):
        for i in range(each):
            high, low = split(x[i])
            blocks[q * each + i, :columns] = high
            blocks[q * each + i, columns:] = low
    for j in range(count):
        for d in range(fan_in):
            picked[j, :, d * width:(d + 1) * width] = blocks[slot_ref[j * fan_in + d]]
    rest = []
    for j in range(count):
        both = half(picked[j], block_of(lower, j), (1, 0))
        both = both[:, :width] + both[:, width:]
        rest.append(sides_ref[j] - (both[:columns] + both[columns:]))
    for j in range(count):
        out_ref[j] = times_turned(rest[j], inverse_ref[j])


def backward_terms(slot_ref, solved, lower, outs, total):
    count, _, width = solved.shape
    fan_in = slot_ref.shape[0] // count
    total[...] = jnp.zeros_like(total)
    for j in range(count):
        terms = times_turned(solved[j], block_of(lower, j))
        for d in range(fan_in):
            slot = slot_ref[j * fan_in + d]
            total[slot] = total[slot] + terms[:, d * width:(d + 1) * width]
    each = outs[0].shape[0]
    for q, out in enumerate(outs):
        out[...] = total[q * each:(q + 1) * each]


def top_kernel(chunks, slot_ref, x0, x1, x2, x3, sides_ref, inverse_ref, *refs):
    lower, outs = refs[:chunks], refs[chunks + 1:chunks + 5]
    sol_ref, (blocks, picked, solved, total) = refs[chunks], refs[chunks + 5:]
    forward_levels(slot_ref, (x0, x1, x2, x3), sides_ref, inverse_ref, lower, solved, blocks, picked)
    for j in range(sol_ref.shape[0]):
        sol_ref[j] = times(solved[j], inverse_ref[j])
    backward_terms(slot_ref, sol_ref, lower, outs, total)


def backward_kernel(chunks, slot_ref, ret0, ret1, forward_ref, inverse_ref, *refs):
    lower, (sol_ref, *outs, total) = refs[:chunks], refs[-6:]
    for j in range(sol_ref.shape[0]):
        sol_ref[j] = times(forward_ref[j] - (ret0[j] + ret1[j]), inverse_ref[j])
    backward_terms(slot_ref, sol_ref, lower, outs, total)


def cut(col_ref, sources, outs, packed):
    share = sources[0].shape[2] // len(outs)
    for level, source in enumerate(sources):
        for c in range(len(outs)):
            packed[c, level] = jnp.concatenate(
                [source[j, :, c * share:(c + 1) * share] for j in range(source.shape[0])], axis=1
            )
    for mask, out in enumerate(outs):
        out[...] = packed[col_ref[0] ^ mask]


def cut_kernel(some, col_ref, *refs):
    cut(col_ref, refs[:some], refs[-5:-1], refs[-1])


def last_kernel(col_ref, ret0, ret1, sides_ref, inverse_ref, *refs):
    outs, (solved, packed) = refs[:-2], refs[-2:]
    for j in range(sides_ref.shape[0]):
        rest = times_turned(sides_ref[j], inverse_ref[j]) - (ret0[j] + ret1[j])
        solved[j] = times(rest, inverse_ref[j])
    cut(col_ref, [solved], outs, packed)


def out_kernel(col_ref, *refs):
    parts, (out_ref, whole) = refs[:-2], refs[-2:]
    levels, count, share, columns = out_ref.shape
    place = 0
    for group in (parts[:4], parts[4:]):
        some, piece, _ = group[0].shape
        for mask, part in enumerate(group):
            start = pl.multiple_of((col_ref[0] ^ mask) * piece, piece)
            for level in range(some):
                whole[place + level, pl.ds(start, piece), :] = part[level]
        place += some
    for level in range(levels):
        out_ref[level] = whole[level].T.reshape(count, share, columns)


def same_kernel(value_ref, *refs):
    refs[-1][...] = value_ref[...]


def after(value, *others):
    return pl.pallas_call(
        same_kernel,
        out_shape=jax.ShapeDtypeStruct(value.shape, value.dtype),
        in_specs=[VMEM] * (1 + len(others)),
        out_specs=VMEM,
        compiler_params=pltpu.CompilerParams(vmem_limit_bytes=8 * 1024 * 1024),
        cost_estimate=TINY,
    )(value, *others)


def pack_kernel(pieces, lower_ref, *refs):
    out_ref, sems = refs[-2:]
    copies, place = [], 0
    for i, (level, start, size) in enumerate(pieces):
        copies.append(
            pltpu.make_async_copy(lower_ref.at[level, pl.ds(start, size)], out_ref.at[pl.ds(place, size)], sems.at[i])
        )
        place += size
    for copy in copies:
        copy.start()
    for copy in copies:
        copy.wait()


def pack(lower_blocks, pieces, *others):
    total = sum(size for _, _, size in pieces)
    return pl.pallas_call(
        functools.partial(pack_kernel, pieces),
        out_shape=jax.ShapeDtypeStruct((total,) + lower_blocks.shape[2:], F32),
        in_specs=[HBM] + [VMEM] * len(others),
        out_specs=VMEM,
        scratch_shapes=[pltpu.SemaphoreType.DMA((len(pieces),))],
        compiler_params=pltpu.CompilerParams(vmem_limit_bytes=8 * 1024 * 1024),
        cost_estimate=TINY,
    )(lower_blocks, *others)


def on_device(right_sides, inverse_diag, lower_blocks, depends_on):
    levels, count, width, columns = right_sides.shape
    share = inverse_diag.shape[2]
    fan_in = lower_blocks.shape[2]
    rows, cols = lax.axis_size("row"), lax.axis_size("col")
    my_row, my_col = lax.axis_index("row"), lax.axis_index("col")
    col = my_col.astype(jnp.int32).reshape(1)
    mine = columns // cols
    entries = count * fan_in
    wanted = lax.dynamic_slice_in_dim(depends_on, my_row * count, count, 1).reshape(levels - 1, entries)
    slots = slot_of((wanted // count) ^ my_row, rows) * count + wanted % count
    slots = [slots[i] for i in range(levels - 1)]

    def like(*shape, dtype=F32):
        return jax.ShapeDtypeStruct(shape, dtype)

    block = like(count, mine, width)
    quarter = like(rows // 4 * count, mine, width)

    def join(level, start, some, parts, place=0):
        own_spec = pl.BlockSpec((None, 1, fan_in, share, width), lambda j: (level, start + j, 0, 0, 0))
        part_spec = pl.BlockSpec((1, fan_in, share, width), lambda j: (place + j, 0, 0, 0))
        out_spec = pl.BlockSpec((1, fan_in * width, 2 * width), lambda j: (j, 0, 0))
        return pl.pallas_call(
            join_kernel,
            grid=(some,),
            out_shape=like(some, fan_in * width, 2 * width, dtype=BF16),
            in_specs=[SMEM, own_spec, own_spec, part_spec, part_spec],
            out_specs=out_spec,
            compiler_params=pltpu.CompilerParams(vmem_limit_bytes=24 * 1024 * 1024),
            cost_estimate=TINY,
        )(col, lower_blocks, lower_beside, *parts)

    def near(value):
        return value, swap(value, "col", 1)

    top = levels - 1
    middle = count // 2
    first, early = call(
        functools.partial(first_kernel, top), [like(count, share, columns), like(middle, fan_in, share, width)], [HBM] * 3,
        scratch=[
            pltpu.VMEM((count, share, width), F32),
            pltpu.VMEM((count, width, columns), F32),
            pltpu.SemaphoreType.DMA((3,)),
        ],
        limit=60,
    )(inverse_diag, right_sides, lower_blocks)
    early = swap(early, "col", 2)
    _, gathered = gather_row(first)
    all_inverse = inverse_diag.reshape(levels * count, share, width)
    parts_inverse = near(all_inverse) + near(swap(all_inverse, "col", 2))
    lower_beside = swap(lower_blocks, "col", 1)

    inverse, token = call(
        join_inverse_kernel, [like(levels * count, width, 2 * width, dtype=BF16), like(8, width)], [SMEM] + [VMEM] * cols
    )(col, *parts_inverse)
    inverse = [inverse[i * count:(i + 1) * count] for i in range(levels)]

    sides = call(
        turn_kernel, like(levels * count, mine, width), [SMEM, VMEM],
        scratch=[pltpu.VMEM((2, columns, width), F32)],
    )(col, right_sides.reshape(levels * count, width, columns))
    sides = [sides[i * count:(i + 1) * count] for i in range(levels)]

    folded, base = call(
        fold_kernel, [like(count, 2 * width, fan_in * share, dtype=BF16), like(count, share, columns)], [HBM] * 3 + [VMEM],
        scratch=[
            pltpu.VMEM(lower_blocks.shape[1:], F32),
            pltpu.VMEM((count, share, width), F32),
            pltpu.VMEM((count, width, columns), F32),
            pltpu.SemaphoreType.DMA((3,)),
        ],
    )(lower_blocks, inverse_diag, right_sides, inverse[1])

    def partial(turn, level, gathered, standing, hold, *others):
        each = count + turn
        kept, passed, sent = call(
            functools.partial(partial_kernel, turn), [like(each, share, columns)] * 2 + [like(2 * each, share, columns)],
            [SMEM] * 2 + [VMEM] * (5 + len(others)),
            scratch=[
                pltpu.VMEM((rows * count, share, 2 * columns), BF16),
                pltpu.VMEM((count, fan_in * share, 2 * columns), BF16),
                pltpu.VMEM((each, width, columns), F32),
            ],
        )(col, slots[level], *gathered, standing, *others)
        beside = swap(sent, "col", 1)
        terms = passed[:count] + beside[each:each + count]
        if turn:
            terms = jnp.concatenate([terms, passed[count:], beside[each + count:]], axis=0)
        return kept, beside[:each], swap(after(terms, hold), "col", 2)

    kept, beside, across = partial(False, 0, gathered, folded, early)
    forward_rows = base - ((kept + beside) + across)
    late = swap(pack(lower_blocks, [(top - 1, middle, count - middle), (1, 0, 1)], across), "col", 2)
    got, gathered = gather_row(forward_rows)

    forward = [None] * levels
    standing = call(
        functools.partial(stand_kernel, 1), like(count, 2 * width, fan_in * share, dtype=BF16), [HBM, VMEM],
        scratch=[pltpu.VMEM(lower_blocks.shape[1:], F32), pltpu.SemaphoreType.DMA],
    )(lower_blocks, got)
    updates = partial(True, 1, gathered, standing, late, forward_rows)
    forward[2], forward[1] = call(
        solve_kernel, [block] * 2, [SMEM] + [VMEM] * 5, scratch=[pltpu.VMEM((cols, mine, width), F32)]
    )(col, *updates, sides[2], inverse[2])
    inner = swap(pack(lower_blocks, [(1, 1, count - 1), (0, 0, middle)], updates[2]), "col", 2)

    picking = [
        pltpu.VMEM((rows * count, 2 * mine, width), BF16),
        pltpu.VMEM((count, 2 * mine, fan_in * width), BF16),
    ]
    total = [pltpu.VMEM((rows * count, mine, width), F32)]

    lower = [None] * (levels - 1)
    got, gathered = gather_row(forward[2])
    early, late = near(early), near(late)
    lower[2] = [join(top - 1, 0, middle, early), join(top - 1, middle, count - middle, late)]
    solved = [None] * levels
    solved[top], *terms = call(
        functools.partial(top_kernel, len(lower[2])), [block] + [quarter] * 4,
        [SMEM] + [VMEM] * 6 + [VMEM] * len(lower[2]),
        scratch=picking + [pltpu.VMEM((count, mine, width), F32)] + total,
    )(slots[2], *gathered, sides[top], inverse[top], *lower[2])
    outer = swap(pack(lower_blocks, [(0, middle, count - middle)], solved[top]), "col", 2)

    got, returned = scatter_row(terms)
    inner = near(after(inner, *got))
    lower[1] = [join(1, 0, 1, late, count - middle), join(1, 1, count - 1, inner)]
    solved[2], *terms = call(
        functools.partial(backward_kernel, 2), [block] + [quarter] * 4, [SMEM] + [VMEM] * 6, scratch=total,
    )(slots[1], *returned, forward[2], inverse[2], *lower[1])

    got, returned = scatter_row(terms)
    lower[0] = [join(0, 0, middle, inner, count - 1), join(0, middle, count - middle, near(after(outer, *got)))]
    solved[1], *terms = call(
        functools.partial(backward_kernel, 2), [block] + [quarter] * 4, [SMEM] + [VMEM] * 6, scratch=total,
    )(slots[0], *returned, forward[1], inverse[1], *lower[0])

    def spread(parts):
        return [parts[0]] + [swap(parts[mask], "col", mask) for mask in range(1, cols)]

    got, returned = scatter_row(terms)
    upper = call(
        functools.partial(cut_kernel, top), [like(top, mine, count * share)] * cols,
        [SMEM] + [VMEM] * (top + len(got)),
        scratch=[pltpu.VMEM((cols, top, mine, count * share), F32)],
    )(col, *solved[1:], *got)
    lowest = call(
        last_kernel, [like(1, mine, count * share)] * cols, [SMEM] + [VMEM] * 4,
        scratch=[
            pltpu.VMEM((count, mine, width), F32),
            pltpu.VMEM((cols, 1, mine, count * share), F32),
        ],
    )(col, *returned, sides[0], inverse[0])
    return call(
        out_kernel, like(levels, count, share, columns), [SMEM] + [VMEM] * (2 * cols),
        scratch=[pltpu.VMEM((levels, columns, count * share), F32)],
    )(col, *spread(lowest), *spread(upper))


def solution(mesh):
    return jax.shard_map(
        on_device,
        mesh=mesh,
        in_specs=(
            P(None, "row", None, None),
            P(None, "row", "col", None),
            P(None, "row", None, "col", None),
            P(),
        ),
        out_specs=P(None, "row", "col", None),
        check_vma=False,
    )
```

```python
import functools

import jax
import jax.numpy as jnp
from jax import lax
from jax.experimental import pallas as pl
from jax.experimental.pallas import tpu as pltpu
from jax.sharding import PartitionSpec as P

F32 = jnp.float32
BF16 = jnp.bfloat16
EXACT = lax.Precision.HIGHEST
VMEM = pl.BlockSpec(memory_space=pltpu.VMEM)
SMEM = pl.BlockSpec(memory_space=pltpu.SMEM)
ANY = pl.BlockSpec(memory_space=pl.ANY)
HBM = pl.BlockSpec(memory_space=pltpu.HBM)
CUTS = (0.625, 0.25, 0.5)
TINY = pl.CostEstimate(flops=1, bytes_accessed=1, transcendentals=0)


def nn(a, b):
    return lax.dot_general(a, b, (((1,), (0,)), ((), ())), precision=EXACT, preferred_element_type=F32)


def half(a, b, contract):
    return lax.dot_general(a, b, ((contract[:1], contract[1:]), ((), ())), preferred_element_type=F32)


def split(value):
    high = value.astype(BF16)
    return high, (value - high.astype(F32)).astype(BF16)


def times(value, pair):
    rows, width = value.shape[0], pair.shape[1] // 2
    both = half(jnp.concatenate(split(value), axis=0), pair, (1, 0))
    both = both[:, :width] + both[:, width:]
    return both[:rows] + both[rows:]


def times_turned(value, pair):
    rows = value.shape[0]
    high, low = split(value)
    wide = jnp.concatenate([jnp.concatenate([high, high], axis=1), jnp.concatenate([low, low], axis=1)], axis=0)
    both = half(wide, pair, (1, 1))
    return both[:rows] + both[rows:]


def call(body, out_shape, in_specs, scratch=(), limit=24):
    return pl.pallas_call(
        body,
        out_shape=out_shape,
        in_specs=in_specs,
        out_specs=jax.tree.map(lambda _: VMEM, out_shape),
        scratch_shapes=list(scratch),
        compiler_params=pltpu.CompilerParams(vmem_limit_bytes=limit * 1024 * 1024),
        cost_estimate=TINY,
    )


def swap(value, axis, mask):
    size = lax.axis_size(axis)
    return lax.ppermute(value, axis, [(i, i ^ mask) for i in range(size)])


def far_masks(size):
    masks, mask = [], size // 2
    while mask >= 4:
        masks.append(mask)
        mask //= 2
    return masks


def slot_of(mask, size):
    place = (mask & 3) * (size // 4)
    for step, far in enumerate(far_masks(size)):
        place = place + jnp.where((mask & far) != 0, 1 << step, 0)
    return place


def gather_row(own):
    held, got = own, own
    for mask in far_masks(lax.axis_size("row")):
        got = swap(held, "row", mask)
        held = jnp.concatenate([held, got], axis=0)
    return got, [held] + [swap(held, "row", mask) for mask in (1, 2, 3)]


def scatter_row(parts):
    total = parts[0]
    got = [swap(part, "row", mask) for mask, part in zip((1, 2, 3), parts[1:])]
    total = total + got[0] + got[1] + got[2]
    other = None
    for mask in reversed(far_masks(lax.axis_size("row"))):
        if other is not None:
            total = total + other
        keep, send = jnp.split(total, 2, axis=0)
        total, other = keep, swap(send, "row", mask)
    return got, (total, other)


def first_kernel(start, inverse_ref, sides_ref, lower_ref, out_ref, early_ref, inverse, sides, sems):
    copies = [
        pltpu.make_async_copy(inverse_ref.at[0], inverse, sems.at[0]),
        pltpu.make_async_copy(sides_ref.at[0], sides, sems.at[1]),
        pltpu.make_async_copy(lower_ref.at[pl.ds(start, early_ref.shape[0])], early_ref, sems.at[2]),
    ]
    for copy in copies:
        copy.start()
    for copy in copies[:2]:
        copy.wait()
    for j in range(out_ref.shape[0]):
        out_ref[j] = nn(inverse[j], sides[j])
    copies[2].wait()


def join_kernel(place, some, col_ref, *refs):
    parts, out_ref = refs[:-1], refs[-1]
    _, share, width = parts[0].shape
    for mask, part in enumerate(parts):
        offset = pl.multiple_of((col_ref[0] ^ mask) * share, share)
        for d in range(some):
            high, low = split(part[place + d])
            out_ref[pl.ds(d * width + offset, share), :width] = high
            out_ref[pl.ds(d * width + offset, share), width:] = low


def join_inverse_kernel(col_ref, *refs):
    parts, (out_ref, token_ref) = refs[:-2], refs[-2:]
    token_ref[...] = jnp.zeros_like(token_ref)
    share, width = parts[0].shape[1:]
    for mask, part in enumerate(parts):
        offset = pl.multiple_of((col_ref[0] ^ mask) * share, share)
        for i in range(part.shape[0]):
            high, low = split(part[i])
            out_ref[i, pl.ds(offset, share), :width] = high
            out_ref[i, pl.ds(offset, share), width:] = low


def stand_kernel(level, col_ref, lower_ref, all_sides_ref, after_ref, out_ref, sides_ref, own, sides, whole, sems):
    count, fan_in, share, width = own.shape
    copies = [
        pltpu.make_async_copy(all_sides_ref, sides, sems.at[0]),
        pltpu.make_async_copy(lower_ref.at[level], own, sems.at[1]),
    ]
    for copy in copies:
        copy.start()
    copies[0].wait()
    start = pl.multiple_of(col_ref[0] * sides_ref.shape[1], sides_ref.shape[1])
    for i in range(sides_ref.shape[0]):
        whole[i % 2] = sides[i // count, i % count].T
        sides_ref[i] = whole[i % 2, pl.ds(start, sides_ref.shape[1]), :]
    copies[1].wait()
    for j in range(count):
        high, low = split(own[j].reshape(fan_in * share, width).T)
        out_ref[j, :width] = high
        out_ref[j, width:] = low


def fold_kernel(lower_ref, own_inverse_ref, sides_ref, inverse_ref, out_ref, base_ref, own, own_inverse, sides, sems):
    count, fan_in, share, width = own.shape
    copies = [
        pltpu.make_async_copy(lower_ref.at[0], own, sems.at[0]),
        pltpu.make_async_copy(own_inverse_ref.at[1], own_inverse, sems.at[1]),
        pltpu.make_async_copy(sides_ref.at[1], sides, sems.at[2]),
    ]
    for copy in copies:
        copy.start()
    for copy in copies:
        copy.wait()
    for j in range(count):
        high, low = split(times_turned(own[j].reshape(fan_in * share, width), inverse_ref[j]).T)
        out_ref[j, :width] = high
        out_ref[j, width:] = low
        base_ref[j] = nn(own_inverse[j], sides[j])


def partial_kernel(turn, col_ref, slot_ref, x0, x1, x2, x3, lower_ref, *refs):
    outs, (blocks, picked, sums) = refs[-6:-3], refs[-3:]
    count = lower_ref.shape[0]
    fan_in = slot_ref.shape[0] // count
    each, share, columns = x0.shape
    width = lower_ref.shape[1] // 2
    for q, x in enumerate((x0, x1, x2, x3)):
        for i in range(each):
            high, low = split(x[i])
            blocks[q * each + i, :, :columns] = high
            blocks[q * each + i, :, columns:] = low
    for j in range(count):
        for d in range(fan_in):
            picked[j, d * share:(d + 1) * share, :] = blocks[slot_ref[j * fan_in + d]]
    for j in range(count):
        both = half(lower_ref[j], picked[j], (1, 0))
        both = both[:width] + both[width:]
        both = both[:, :columns] + both[:, columns:]
        sums[j] = both.T if turn else both
    each, piece, _ = outs[0].shape
    if turn:
        sums[count] = refs[0][...].reshape(count * share, columns).T
    for place, mask in enumerate((0, 2, 1, 3)):
        start = pl.multiple_of((col_ref[0] ^ mask) * piece, piece)
        out = outs[place] if place < 2 else outs[2].at[pl.ds((place - 2) * each, each)]
        for j in range(each):
            out[j] = sums[j, pl.ds(start, piece), :]


def solve_kernel(col_ref, u0, u1, u2, sides_ref, inverse_ref, out_ref, lower_ref, parts):
    count = out_ref.shape[0]
    share = u0.shape[2] // count
    for j in range(count):
        out_ref[j] = times_turned(sides_ref[j] - ((u0[j] + u1[j]) + u2[j]), inverse_ref[j])
    parts[0], parts[1], parts[2], parts[3] = u0[count], u1[count], u2[count], u2[count + 1]
    for c in range(parts.shape[0]):
        part = parts[col_ref[0] ^ c]
        for j in range(count):
            lower_ref[j, :, c * share:(c + 1) * share] = part[:, j * share:(j + 1) * share]


def runs_of(spans, lower, j, fan_in):
    width = lower[0].shape[1] // 2
    for (start, end), ref in zip(spans, lower):
        low, high = max(start, j * fan_in), min(end, (j + 1) * fan_in)
        if low < high:
            yield low - j * fan_in, high - j * fan_in, ref[(low - start) * width:(high - start) * width, :]


def forward_levels(spans, slot_ref, xs, sides_ref, inverse_ref, lower, out_ref, blocks, picked):
    count, columns, width = out_ref.shape
    fan_in = slot_ref.shape[0] // count
    each = xs[0].shape[0]
    for q, x in enumerate(xs):
        for i in range(each):
            high, low = split(x[i])
            blocks[q * each + i, :columns] = high
            blocks[q * each + i, columns:] = low
    for j in range(count):
        for d in range(fan_in):
            picked[j, :, d * width:(d + 1) * width] = blocks[slot_ref[j * fan_in + d]]
    rest = []
    for j in range(count):
        value = sides_ref[j]
        for low, high, rows in runs_of(spans, lower, j, fan_in):
            both = half(picked[j, :, low * width:high * width], rows, (1, 0))
            both = both[:, :width] + both[:, width:]
            value = value - (both[:columns] + both[columns:])
        rest.append(value)
    for j in range(count):
        out_ref[j] = times_turned(rest[j], inverse_ref[j])


def backward_terms(spans, slot_ref, solved, lower, outs, total):
    count, _, width = solved.shape
    fan_in = slot_ref.shape[0] // count
    total[...] = jnp.zeros_like(total)
    for j in range(count):
        for low, high, rows in runs_of(spans, lower, j, fan_in):
            terms = times_turned(solved[j], rows)
            for d in range(low, high):
                slot = slot_ref[j * fan_in + d]
                total[slot] = total[slot] + terms[:, (d - low) * width:(d - low + 1) * width]
    each = outs[0].shape[0]
    for q, out in enumerate(outs):
        out[...] = total[q * each:(q + 1) * each]


def top_kernel(spans, slot_ref, x0, x1, x2, x3, sides_ref, inverse_ref, *refs):
    chunks = len(spans)
    lower, outs = refs[:chunks], refs[chunks + 1:chunks + 5]
    sol_ref, (blocks, picked, solved, total) = refs[chunks], refs[chunks + 5:]
    forward_levels(spans, slot_ref, (x0, x1, x2, x3), sides_ref, inverse_ref, lower, solved, blocks, picked)
    for j in range(sol_ref.shape[0]):
        sol_ref[j] = times(solved[j], inverse_ref[j])
    backward_terms(spans, slot_ref, sol_ref, lower, outs, total)


def backward_kernel(spans, slot_ref, ret0, ret1, forward_ref, inverse_ref, *refs):
    lower, (sol_ref, *outs, total) = refs[:len(spans)], refs[-6:]
    for j in range(sol_ref.shape[0]):
        sol_ref[j] = times(forward_ref[j] - (ret0[j] + ret1[j]), inverse_ref[j])
    backward_terms(spans, slot_ref, sol_ref, lower, outs, total)


def cut(col_ref, sources, outs, packed):
    share = sources[0].shape[2] // len(outs)
    for level, source in enumerate(sources):
        for c in range(len(outs)):
            packed[c, level] = jnp.concatenate(
                [source[j, :, c * share:(c + 1) * share] for j in range(source.shape[0])], axis=1
            )
    for mask, out in enumerate(outs):
        out[...] = packed[col_ref[0] ^ mask]


def cut_kernel(some, col_ref, *refs):
    cut(col_ref, refs[:some], refs[-5:-1], refs[-1])


def last_kernel(col_ref, ret0, ret1, sides_ref, inverse_ref, *refs):
    outs, (solved, packed) = refs[:-2], refs[-2:]
    for j in range(sides_ref.shape[0]):
        rest = times_turned(sides_ref[j], inverse_ref[j]) - (ret0[j] + ret1[j])
        solved[j] = times(rest, inverse_ref[j])
    cut(col_ref, [solved], outs, packed)


def out_kernel(col_ref, *refs):
    parts, (out_ref, whole) = refs[:-2], refs[-2:]
    levels, count, share, columns = out_ref.shape
    place = 0
    for group in (parts[:4], parts[4:]):
        some, piece, _ = group[0].shape
        for mask, part in enumerate(group):
            start = pl.multiple_of((col_ref[0] ^ mask) * piece, piece)
            for level in range(some):
                whole[place + level, pl.ds(start, piece), :] = part[level]
        place += some
    for level in range(levels):
        out_ref[level] = whole[level].T.reshape(count, share, columns)


def same_kernel(value_ref, *refs):
    refs[-1][...] = value_ref[...]


def after(value, *others, spec=VMEM):
    return pl.pallas_call(
        same_kernel,
        out_shape=jax.ShapeDtypeStruct(value.shape, value.dtype),
        in_specs=[VMEM] + [spec] * len(others),
        out_specs=VMEM,
        compiler_params=pltpu.CompilerParams(vmem_limit_bytes=8 * 1024 * 1024),
        cost_estimate=TINY,
    )(value, *others)


def pack_kernel(pieces, lower_ref, *refs):
    out_ref, sems = refs[-2:]
    copies, place = [], 0
    for i, (start, size) in enumerate(pieces):
        copies.append(pltpu.make_async_copy(lower_ref.at[pl.ds(start, size)], out_ref.at[pl.ds(place, size)], sems.at[i]))
        place += size
    for copy in copies:
        copy.start()
    for copy in copies:
        copy.wait()


def pack(blocks, pieces, *others):
    total = sum(size for _, size in pieces)
    return pl.pallas_call(
        functools.partial(pack_kernel, pieces),
        out_shape=jax.ShapeDtypeStruct((total,) + blocks.shape[1:], F32),
        in_specs=[HBM] + [VMEM] * len(others),
        out_specs=VMEM,
        scratch_shapes=[pltpu.SemaphoreType.DMA((len(pieces),))],
        compiler_params=pltpu.CompilerParams(vmem_limit_bytes=8 * 1024 * 1024),
        cost_estimate=TINY,
    )(blocks, *others)


def on_device(right_sides, inverse_diag, lower_blocks, depends_on):
    levels, count, width, columns = right_sides.shape
    share = inverse_diag.shape[2]
    fan_in = lower_blocks.shape[2]
    rows, cols = lax.axis_size("row"), lax.axis_size("col")
    my_row, my_col = lax.axis_index("row"), lax.axis_index("col")
    col = my_col.astype(jnp.int32).reshape(1)
    mine = columns // cols
    entries = count * fan_in
    wanted = lax.dynamic_slice_in_dim(depends_on, my_row * count, count, 1).reshape(levels - 1, entries)
    slots = slot_of((wanted // count) ^ my_row, rows) * count + wanted % count
    slots = [slots[i] for i in range(levels - 1)]

    def like(*shape, dtype=F32):
        return jax.ShapeDtypeStruct(shape, dtype)

    block = like(count, mine, width)
    quarter = like(rows // 4 * count, mine, width)

    def join(parts, place, some):
        return call(
            functools.partial(join_kernel, place, some), like(some * width, 2 * width, dtype=BF16), [SMEM] + [VMEM] * cols
        )(col, *parts)

    def near(value):
        return value, swap(value, "col", 1)

    top = levels - 1
    flat = lower_blocks.reshape((levels - 1) * entries, share, width)
    unit = fan_in // 2
    cuts = [int(entries * part) // unit * unit for part in CUTS]
    spans = [((0, cut), (cut, entries)) for cut in cuts]
    at2, at1, at0 = (top - 1) * entries, (top - 2) * entries, (top - 3) * entries
    first, early = call(
        functools.partial(first_kernel, at2), [like(count, share, columns), like(cuts[0], share, width)], [HBM] * 3,
        scratch=[
            pltpu.VMEM((count, share, width), F32),
            pltpu.VMEM((count, width, columns), F32),
            pltpu.SemaphoreType.DMA((3,)),
        ],
        limit=60,
    )(inverse_diag, right_sides, flat)
    early = near(early) + (swap(early, "col", 2),)
    _, gathered = gather_row(first)
    all_inverse = inverse_diag.reshape(levels * count, share, width)
    parts_inverse = near(all_inverse) + near(swap(all_inverse, "col", 2))

    inverse, token = call(
        join_inverse_kernel, [like(levels * count, width, 2 * width, dtype=BF16), like(8, width)], [SMEM] + [VMEM] * cols
    )(col, *parts_inverse)
    inverse = [inverse[i * count:(i + 1) * count] for i in range(levels)]

    folded, base = call(
        fold_kernel, [like(count, 2 * width, fan_in * share, dtype=BF16), like(count, share, columns)], [HBM] * 3 + [VMEM],
        scratch=[
            pltpu.VMEM(lower_blocks.shape[1:], F32),
            pltpu.VMEM((count, share, width), F32),
            pltpu.VMEM((count, width, columns), F32),
            pltpu.SemaphoreType.DMA((3,)),
        ],
    )(lower_blocks, inverse_diag, right_sides, inverse[1])

    def partial(turn, level, gathered, standing, hold, *others):
        each = count + turn
        kept, passed, sent = call(
            functools.partial(partial_kernel, turn), [like(each, share, columns)] * 2 + [like(2 * each, share, columns)],
            [SMEM] * 2 + [VMEM] * (5 + len(others)),
            scratch=[
                pltpu.VMEM((rows * count, share, 2 * columns), BF16),
                pltpu.VMEM((count, fan_in * share, 2 * columns), BF16),
                pltpu.VMEM((each, width, columns), F32),
            ],
        )(col, slots[level], *gathered, standing, *others)
        beside = swap(sent, "col", 1)
        terms = passed[:count] + beside[each:each + count]
        if turn:
            terms = jnp.concatenate([terms, passed[count:], beside[each + count:]], axis=0)
        return kept, beside[:each], swap(after(terms, hold, spec=VMEM if turn else ANY), "col", 2)

    kept, beside, across = partial(False, 0, gathered, folded, early[2])
    forward_rows = base - ((kept + beside) + across)
    late = pack(flat, [(at2 + cuts[0], entries - cuts[0]), (at1, cuts[1])], across)
    late = near(late) + (swap(late, "col", 2),)
    got, gathered = gather_row(forward_rows)

    forward = [None] * levels
    standing, sides = call(
        functools.partial(stand_kernel, 1),
        [like(count, 2 * width, fan_in * share, dtype=BF16), like(levels * count, mine, width)],
        [SMEM, HBM, HBM, VMEM],
        scratch=[
            pltpu.VMEM(lower_blocks.shape[1:], F32),
            pltpu.VMEM(right_sides.shape, F32),
            pltpu.VMEM((2, columns, width), F32),
            pltpu.SemaphoreType.DMA((2,)),
        ],
    )(col, lower_blocks, right_sides, got)
    sides = [sides[i * count:(i + 1) * count] for i in range(levels)]
    updates = partial(True, 1, gathered, standing, late[2], forward_rows)
    forward[2], forward[1] = call(
        solve_kernel, [block] * 2, [SMEM] + [VMEM] * 5, scratch=[pltpu.VMEM((cols, mine, width), F32)]
    )(col, *updates, sides[2], inverse[2])
    inner = pack(flat, [(at1 + cuts[1], entries - cuts[1]), (at0, cuts[2])], updates[2])
    inner_across = swap(inner, "col", 2)

    picking = [
        pltpu.VMEM((rows * count, 2 * mine, width), BF16),
        pltpu.VMEM((count, 2 * mine, fan_in * width), BF16),
    ]
    total = [pltpu.VMEM((rows * count, mine, width), F32)]

    lower = [None] * (levels - 1)
    got, gathered = gather_row(forward[2])
    early, late = early[:2] + near(early[2]), late[:2] + near(late[2])
    lower[2] = [join(early, 0, cuts[0]), join(late, 0, entries - cuts[0])]
    solved = [None] * levels
    solved[top], *terms = call(
        functools.partial(top_kernel, spans[0]), [block] + [quarter] * 4,
        [SMEM] + [VMEM] * 6 + [VMEM] * len(lower[2]),
        scratch=picking + [pltpu.VMEM((count, mine, width), F32)] + total,
    )(slots[2], *gathered, sides[top], inverse[top], *lower[2])
    outer = pack(flat, [(at0 + cuts[2], entries - cuts[2])], solved[top])
    outer_across = swap(outer, "col", 2)

    got, returned = scatter_row(terms)
    inner = near(inner) + near(after(inner_across, *got))
    lower[1] = [join(late, entries - cuts[0], cuts[1]), join(inner, 0, entries - cuts[1])]
    solved[2], *terms = call(
        functools.partial(backward_kernel, spans[1]), [block] + [quarter] * 4, [SMEM] + [VMEM] * 6, scratch=total,
    )(slots[1], *returned, forward[2], inverse[2], *lower[1])

    got, returned = scatter_row(terms)
    outer = near(outer) + near(after(outer_across, *got))
    lower[0] = [join(inner, entries - cuts[1], cuts[2]), join(outer, 0, entries - cuts[2])]
    solved[1], *terms = call(
        functools.partial(backward_kernel, spans[2]), [block] + [quarter] * 4, [SMEM] + [VMEM] * 6, scratch=total,
    )(slots[0], *returned, forward[1], inverse[1], *lower[0])

    def spread(parts):
        return [parts[0]] + [swap(parts[mask], "col", mask) for mask in range(1, cols)]

    got, returned = scatter_row(terms)
    upper = call(
        functools.partial(cut_kernel, top), [like(top, mine, count * share)] * cols,
        [SMEM] + [VMEM] * (top + len(got)),
        scratch=[pltpu.VMEM((cols, top, mine, count * share), F32)],
    )(col, *solved[1:], *got)
    lowest = call(
        last_kernel, [like(1, mine, count * share)] * cols, [SMEM] + [VMEM] * 4,
        scratch=[
            pltpu.VMEM((count, mine, width), F32),
            pltpu.VMEM((cols, 1, mine, count * share), F32),
        ],
    )(col, *returned, sides[0], inverse[0])
    return call(
        out_kernel, like(levels, count, share, columns), [SMEM] + [VMEM] * (2 * cols),
        scratch=[pltpu.VMEM((levels, columns, count * share), F32)],
    )(col, *spread(lowest), *spread(upper))


def solution(mesh):
    return jax.shard_map(
        on_device,
        mesh=mesh,
        in_specs=(
            P(None, "row", None, None),
            P(None, "row", "col", None),
            P(None, "row", None, "col", None),
            P(),
        ),
        out_specs=P(None, "row", "col", None),
        check_vma=False,
    )
```

```python
import functools

import jax
import jax.numpy as jnp
from jax import lax
from jax.experimental import pallas as pl
from jax.experimental.pallas import tpu as pltpu
from jax.sharding import PartitionSpec as P

F32 = jnp.float32
BF16 = jnp.bfloat16
EXACT = lax.Precision.HIGHEST
VMEM = pl.BlockSpec(memory_space=pltpu.VMEM)
SMEM = pl.BlockSpec(memory_space=pltpu.SMEM)
ANY = pl.BlockSpec(memory_space=pl.ANY)
HBM = pl.BlockSpec(memory_space=pltpu.HBM)
CUTS = (0.625, 0.25, 0.5)
TINY = pl.CostEstimate(flops=1, bytes_accessed=1, transcendentals=0)


def nn(a, b):
    return lax.dot_general(a, b, (((1,), (0,)), ((), ())), precision=EXACT, preferred_element_type=F32)


def half(a, b, contract):
    return lax.dot_general(a, b, ((contract[:1], contract[1:]), ((), ())), preferred_element_type=F32)


def split(value):
    high = value.astype(BF16)
    return high, (value - high.astype(F32)).astype(BF16)


def times(value, pair):
    rows, width = value.shape[0], pair.shape[1] // 2
    both = half(jnp.concatenate(split(value), axis=0), pair, (1, 0))
    both = both[:, :width] + both[:, width:]
    return both[:rows] + both[rows:]


def times_turned(value, pair):
    rows = value.shape[0]
    high, low = split(value)
    wide = jnp.concatenate([jnp.concatenate([high, high], axis=1), jnp.concatenate([low, low], axis=1)], axis=0)
    both = half(wide, pair, (1, 1))
    return both[:rows] + both[rows:]


def call(body, out_shape, in_specs, scratch=(), limit=24):
    return pl.pallas_call(
        body,
        out_shape=out_shape,
        in_specs=in_specs,
        out_specs=jax.tree.map(lambda _: VMEM, out_shape),
        scratch_shapes=list(scratch),
        compiler_params=pltpu.CompilerParams(vmem_limit_bytes=limit * 1024 * 1024),
        cost_estimate=TINY,
    )


def swap(value, axis, mask):
    size = lax.axis_size(axis)
    return lax.ppermute(value, axis, [(i, i ^ mask) for i in range(size)])


def far_masks(size):
    masks, mask = [], size // 2
    while mask >= 4:
        masks.append(mask)
        mask //= 2
    return masks


def slot_of(mask, size):
    place = (mask & 3) * (size // 4)
    for step, far in enumerate(far_masks(size)):
        place = place + jnp.where((mask & far) != 0, 1 << step, 0)
    return place


def gather_row(own):
    held, got = own, own
    for mask in far_masks(lax.axis_size("row")):
        got = swap(held, "row", mask)
        held = jnp.concatenate([held, got], axis=0)
    return got, [held] + [swap(held, "row", mask) for mask in (1, 2, 3)]


def scatter_row(parts):
    total = parts[0]
    got = [swap(part, "row", mask) for mask, part in zip((1, 2, 3), parts[1:])]
    total = total + got[0] + got[1] + got[2]
    other = None
    for mask in reversed(far_masks(lax.axis_size("row"))):
        if other is not None:
            total = total + other
        keep, send = jnp.split(total, 2, axis=0)
        total, other = keep, swap(send, "row", mask)
    return got, (total, other)


def first_kernel(start, inverse_ref, sides_ref, lower_ref, out_ref, early_ref, inverse, sides, sems):
    copies = [
        pltpu.make_async_copy(inverse_ref.at[0], inverse, sems.at[0]),
        pltpu.make_async_copy(sides_ref.at[0], sides, sems.at[1]),
        pltpu.make_async_copy(lower_ref.at[pl.ds(start, early_ref.shape[0])], early_ref, sems.at[2]),
    ]
    for copy in copies:
        copy.start()
    for copy in copies[:2]:
        copy.wait()
    for j in range(out_ref.shape[0]):
        out_ref[j] = nn(inverse[j], sides[j])
    copies[2].wait()


def join_kernel(place, some, col_ref, *refs):
    parts, out_ref = refs[:-1], refs[-1]
    _, share, width = parts[0].shape
    for mask, part in enumerate(parts):
        offset = pl.multiple_of((col_ref[0] ^ mask) * share, share)
        for d in range(some):
            high, low = split(part[place + d])
            out_ref[pl.ds(d * width + offset, share), :width] = high
            out_ref[pl.ds(d * width + offset, share), width:] = low


def join_inverse_kernel(col_ref, *refs):
    parts, (out_ref, token_ref) = refs[:-2], refs[-2:]
    token_ref[...] = jnp.zeros_like(token_ref)
    share, width = parts[0].shape[1:]
    for mask, part in enumerate(parts):
        offset = pl.multiple_of((col_ref[0] ^ mask) * share, share)
        for i in range(part.shape[0]):
            high, low = split(part[i])
            out_ref[i, pl.ds(offset, share), :width] = high
            out_ref[i, pl.ds(offset, share), width:] = low


def stand_kernel(level, col_ref, lower_ref, all_sides_ref, after_ref, out_ref, sides_ref, own, sides, whole, sems):
    count, fan_in, share, width = own.shape
    copies = [
        pltpu.make_async_copy(all_sides_ref, sides, sems.at[0]),
        pltpu.make_async_copy(lower_ref.at[level], own, sems.at[1]),
    ]
    for copy in copies:
        copy.start()
    copies[0].wait()
    start = pl.multiple_of(col_ref[0] * sides_ref.shape[1], sides_ref.shape[1])
    for i in range(sides_ref.shape[0]):
        whole[i % 2] = sides[i // count, i % count].T
        sides_ref[i] = whole[i % 2, pl.ds(start, sides_ref.shape[1]), :]
    copies[1].wait()
    for j in range(count):
        high, low = split(own[j].reshape(fan_in * share, width).T)
        out_ref[j, :width] = high
        out_ref[j, width:] = low


def fold_kernel(lower_ref, own_inverse_ref, sides_ref, inverse_ref, out_ref, base_ref, own, own_inverse, sides, sems):
    count, fan_in, share, width = own.shape
    copies = [
        pltpu.make_async_copy(lower_ref.at[0], own, sems.at[0]),
        pltpu.make_async_copy(own_inverse_ref.at[1], own_inverse, sems.at[1]),
        pltpu.make_async_copy(sides_ref.at[1], sides, sems.at[2]),
    ]
    for copy in copies:
        copy.start()
    for copy in copies:
        copy.wait()
    for j in range(count):
        high, low = split(times_turned(own[j].reshape(fan_in * share, width), inverse_ref[j]).T)
        out_ref[j, :width] = high
        out_ref[j, width:] = low
        base_ref[j] = nn(own_inverse[j], sides[j])


def partial_kernel(turn, col_ref, slot_ref, x0, x1, x2, x3, lower_ref, *refs):
    outs, (blocks, picked, sums) = refs[-6:-3], refs[-3:]
    count = lower_ref.shape[0]
    fan_in = slot_ref.shape[0] // count
    each, share, columns = x0.shape
    width = lower_ref.shape[1] // 2
    for q, x in enumerate((x0, x1, x2, x3)):
        for i in range(each):
            high, low = split(x[i])
            blocks[q * each + i, :, :columns] = high
            blocks[q * each + i, :, columns:] = low
    for j in range(count):
        for d in range(fan_in):
            picked[j, d * share:(d + 1) * share, :] = blocks[slot_ref[j * fan_in + d]]
    for j in range(count):
        both = half(lower_ref[j], picked[j], (1, 0))
        both = both[:width] + both[width:]
        both = both[:, :columns] + both[:, columns:]
        sums[j] = both.T if turn else both
    each, piece, _ = outs[0].shape
    if turn:
        sums[count] = refs[0][...].reshape(count * share, columns).T
    for place, mask in enumerate((0, 2, 1, 3)):
        start = pl.multiple_of((col_ref[0] ^ mask) * piece, piece)
        out = outs[place] if place < 2 else outs[2].at[pl.ds((place - 2) * each, each)]
        for j in range(each):
            out[j] = sums[j, pl.ds(start, piece), :]


def solve_kernel(col_ref, u0, u1, u2, sides_ref, inverse_ref, out_ref, lower_ref, parts):
    count = out_ref.shape[0]
    share = u0.shape[2] // count
    for j in range(count):
        out_ref[j] = times_turned(sides_ref[j] - ((u0[j] + u1[j]) + u2[j]), inverse_ref[j])
    parts[0], parts[1], parts[2], parts[3] = u0[count], u1[count], u2[count], u2[count + 1]
    for c in range(parts.shape[0]):
        part = parts[col_ref[0] ^ c]
        for j in range(count):
            lower_ref[j, :, c * share:(c + 1) * share] = part[:, j * share:(j + 1) * share]


def runs_of(spans, lower, j, fan_in):
    width = lower[0].shape[1] // 2
    for (start, end), ref in zip(spans, lower):
        low, high = max(start, j * fan_in), min(end, (j + 1) * fan_in)
        if low < high:
            yield low - j * fan_in, high - j * fan_in, ref[(low - start) * width:(high - start) * width, :]


def forward_levels(spans, slot_ref, xs, sides_ref, inverse_ref, lower, out_ref, blocks, picked):
    count, columns, width = out_ref.shape
    fan_in = slot_ref.shape[0] // count
    each = xs[0].shape[0]
    for q, x in enumerate(xs):
        for i in range(each):
            high, low = split(x[i])
            blocks[q * each + i, :columns] = high
            blocks[q * each + i, columns:] = low
    for j in range(count):
        for d in range(fan_in):
            picked[j, :, d * width:(d + 1) * width] = blocks[slot_ref[j * fan_in + d]]
    rest = []
    for j in range(count):
        value = sides_ref[j]
        for low, high, rows in runs_of(spans, lower, j, fan_in):
            both = half(picked[j, :, low * width:high * width], rows, (1, 0))
            both = both[:, :width] + both[:, width:]
            value = value - (both[:columns] + both[columns:])
        rest.append(value)
    for j in range(count):
        out_ref[j] = times_turned(rest[j], inverse_ref[j])


def backward_terms(spans, slot_ref, solved, lower, outs, total):
    count, _, width = solved.shape
    fan_in = slot_ref.shape[0] // count
    total[...] = jnp.zeros_like(total)
    for j in range(count):
        for low, high, rows in runs_of(spans, lower, j, fan_in):
            terms = times_turned(solved[j], rows)
            for d in range(low, high):
                slot = slot_ref[j * fan_in + d]
                total[slot] = total[slot] + terms[:, (d - low) * width:(d - low + 1) * width]
    each = outs[0].shape[0]
    for q, out in enumerate(outs):
        out[...] = total[q * each:(q + 1) * each]


def top_kernel(spans, slot_ref, x0, x1, x2, x3, sides_ref, inverse_ref, *refs):
    chunks = len(spans)
    lower, outs = refs[:chunks], refs[chunks + 1:chunks + 5]
    sol_ref, (blocks, picked, solved, total) = refs[chunks], refs[chunks + 5:]
    forward_levels(spans, slot_ref, (x0, x1, x2, x3), sides_ref, inverse_ref, lower, solved, blocks, picked)
    for j in range(sol_ref.shape[0]):
        sol_ref[j] = times(solved[j], inverse_ref[j])
    backward_terms(spans, slot_ref, sol_ref, lower, outs, total)


def backward_kernel(spans, slot_ref, ret0, ret1, forward_ref, inverse_ref, *refs):
    lower, (sol_ref, *outs, total) = refs[:len(spans)], refs[-6:]
    for j in range(sol_ref.shape[0]):
        sol_ref[j] = times(forward_ref[j] - (ret0[j] + ret1[j]), inverse_ref[j])
    backward_terms(spans, slot_ref, sol_ref, lower, outs, total)


def cut(col_ref, sources, outs, packed):
    share = sources[0].shape[2] // len(outs)
    for level, source in enumerate(sources):
        for c in range(len(outs)):
            packed[c, level] = jnp.concatenate(
                [source[j, :, c * share:(c + 1) * share] for j in range(source.shape[0])], axis=1
            )
    for mask, out in enumerate(outs):
        out[...] = packed[col_ref[0] ^ mask]


def cut_kernel(some, col_ref, *refs):
    cut(col_ref, refs[:some], refs[-5:-1], refs[-1])


def ahead_kernel(ret_ref, sides_ref, inverse_ref, out_ref):
    for j in range(out_ref.shape[0]):
        out_ref[j] = times(times_turned(sides_ref[j], inverse_ref[j]) - ret_ref[j], inverse_ref[j])


def last_kernel(col_ref, ret_ref, ahead_ref, inverse_ref, *refs):
    outs, (solved, packed) = refs[:-2], refs[-2:]
    for j in range(ahead_ref.shape[0]):
        solved[j] = ahead_ref[j] - times(ret_ref[j], inverse_ref[j])
    cut(col_ref, [solved], outs, packed)


def place(col_ref, parts, whole, outs):
    some, piece, columns = parts[0].shape
    for mask, part in enumerate(parts):
        start = pl.multiple_of((col_ref[0] ^ mask) * piece, piece)
        for level in range(some):
            whole[level, pl.ds(start, piece), :] = part[level]
    for level in range(some):
        outs[level] = whole[level].T.reshape(outs.shape[1:])


def upper_kernel(col_ref, *refs):
    place(col_ref, refs[:4], refs[5], refs[4])


def out_kernel(col_ref, *refs):
    parts, (upper_ref, out_ref, whole, lowest, sems) = refs[:4], refs[4:]
    above = pltpu.make_async_copy(upper_ref, out_ref.at[pl.ds(1, upper_ref.shape[0])], sems.at[0])
    above.start()
    place(col_ref, parts, whole, lowest)
    below = pltpu.make_async_copy(lowest, out_ref.at[pl.ds(0, 1)], sems.at[1])
    below.start()
    above.wait()
    below.wait()


def same_kernel(value_ref, *refs):
    refs[-1][...] = value_ref[...]


def after(value, *others, spec=VMEM):
    return pl.pallas_call(
        same_kernel,
        out_shape=jax.ShapeDtypeStruct(value.shape, value.dtype),
        in_specs=[VMEM] + [spec] * len(others),
        out_specs=VMEM,
        compiler_params=pltpu.CompilerParams(vmem_limit_bytes=8 * 1024 * 1024),
        cost_estimate=TINY,
    )(value, *others)


def pack_kernel(pieces, lower_ref, *refs):
    out_ref, sems = refs[-2:]
    copies, place = [], 0
    for i, (start, size) in enumerate(pieces):
        copies.append(pltpu.make_async_copy(lower_ref.at[pl.ds(start, size)], out_ref.at[pl.ds(place, size)], sems.at[i]))
        place += size
    for copy in copies:
        copy.start()
    for copy in copies:
        copy.wait()


def pack(blocks, pieces, *others):
    total = sum(size for _, size in pieces)
    return pl.pallas_call(
        functools.partial(pack_kernel, pieces),
        out_shape=jax.ShapeDtypeStruct((total,) + blocks.shape[1:], F32),
        in_specs=[HBM] + [VMEM] * len(others),
        out_specs=VMEM,
        scratch_shapes=[pltpu.SemaphoreType.DMA((len(pieces),))],
        compiler_params=pltpu.CompilerParams(vmem_limit_bytes=8 * 1024 * 1024),
        cost_estimate=TINY,
    )(blocks, *others)


def on_device(right_sides, inverse_diag, lower_blocks, depends_on):
    levels, count, width, columns = right_sides.shape
    share = inverse_diag.shape[2]
    fan_in = lower_blocks.shape[2]
    rows, cols = lax.axis_size("row"), lax.axis_size("col")
    my_row, my_col = lax.axis_index("row"), lax.axis_index("col")
    col = my_col.astype(jnp.int32).reshape(1)
    mine = columns // cols
    entries = count * fan_in
    wanted = lax.dynamic_slice_in_dim(depends_on, my_row * count, count, 1).reshape(levels - 1, entries)
    slots = slot_of((wanted // count) ^ my_row, rows) * count + wanted % count
    slots = [slots[i] for i in range(levels - 1)]

    def like(*shape, dtype=F32):
        return jax.ShapeDtypeStruct(shape, dtype)

    block = like(count, mine, width)
    quarter = like(rows // 4 * count, mine, width)

    def join(parts, place, some):
        return call(
            functools.partial(join_kernel, place, some), like(some * width, 2 * width, dtype=BF16), [SMEM] + [VMEM] * cols
        )(col, *parts)

    def near(value):
        return value, swap(value, "col", 1)

    top = levels - 1
    flat = lower_blocks.reshape((levels - 1) * entries, share, width)
    unit = fan_in // 2
    cuts = [int(entries * part) // unit * unit for part in CUTS]
    spans = [((0, cut), (cut, entries)) for cut in cuts]
    at2, at1, at0 = (top - 1) * entries, (top - 2) * entries, (top - 3) * entries
    first, early = call(
        functools.partial(first_kernel, at2), [like(count, share, columns), like(cuts[0], share, width)], [HBM] * 3,
        scratch=[
            pltpu.VMEM((count, share, width), F32),
            pltpu.VMEM((count, width, columns), F32),
            pltpu.SemaphoreType.DMA((3,)),
        ],
        limit=60,
    )(inverse_diag, right_sides, flat)
    early = near(early) + (swap(early, "col", 2),)
    _, gathered = gather_row(first)
    all_inverse = inverse_diag.reshape(levels * count, share, width)
    parts_inverse = (all_inverse, swap(after(all_inverse, first), "col", 1)) + near(swap(all_inverse, "col", 2))

    inverse, token = call(
        join_inverse_kernel, [like(levels * count, width, 2 * width, dtype=BF16), like(8, width)], [SMEM] + [VMEM] * cols
    )(col, *parts_inverse)
    inverse = [inverse[i * count:(i + 1) * count] for i in range(levels)]

    folded, base = call(
        fold_kernel, [like(count, 2 * width, fan_in * share, dtype=BF16), like(count, share, columns)], [HBM] * 3 + [VMEM],
        scratch=[
            pltpu.VMEM(lower_blocks.shape[1:], F32),
            pltpu.VMEM((count, share, width), F32),
            pltpu.VMEM((count, width, columns), F32),
            pltpu.SemaphoreType.DMA((3,)),
        ],
    )(lower_blocks, inverse_diag, right_sides, inverse[1])

    def partial(turn, level, gathered, standing, hold, *others):
        each = count + turn
        kept, passed, sent = call(
            functools.partial(partial_kernel, turn), [like(each, share, columns)] * 2 + [like(2 * each, share, columns)],
            [SMEM] * 2 + [VMEM] * (5 + len(others)),
            scratch=[
                pltpu.VMEM((rows * count, share, 2 * columns), BF16),
                pltpu.VMEM((count, fan_in * share, 2 * columns), BF16),
                pltpu.VMEM((each, width, columns), F32),
            ],
        )(col, slots[level], *gathered, standing, *others)
        beside = swap(sent, "col", 1)
        terms = passed[:count] + beside[each:each + count]
        if turn:
            terms = jnp.concatenate([terms, passed[count:], beside[each + count:]], axis=0)
        return kept, beside[:each], swap(after(terms, hold, spec=VMEM if turn else ANY), "col", 2)

    kept, beside, across = partial(False, 0, gathered, folded, early[2])
    forward_rows = base - ((kept + beside) + across)
    late = pack(flat, [(at2 + cuts[0], entries - cuts[0]), (at1, cuts[1])], across)
    late = near(late) + (swap(late, "col", 2),)
    got, gathered = gather_row(forward_rows)

    forward = [None] * levels
    standing, sides = call(
        functools.partial(stand_kernel, 1),
        [like(count, 2 * width, fan_in * share, dtype=BF16), like(levels * count, mine, width)],
        [SMEM, HBM, HBM, VMEM],
        scratch=[
            pltpu.VMEM(lower_blocks.shape[1:], F32),
            pltpu.VMEM(right_sides.shape, F32),
            pltpu.VMEM((2, columns, width), F32),
            pltpu.SemaphoreType.DMA((2,)),
        ],
    )(col, lower_blocks, right_sides, got)
    sides = [sides[i * count:(i + 1) * count] for i in range(levels)]
    updates = partial(True, 1, gathered, standing, late[2], forward_rows)
    forward[2], forward[1] = call(
        solve_kernel, [block] * 2, [SMEM] + [VMEM] * 5, scratch=[pltpu.VMEM((cols, mine, width), F32)]
    )(col, *updates, sides[2], inverse[2])
    inner = pack(flat, [(at1 + cuts[1], entries - cuts[1]), (at0, cuts[2])], updates[2])
    inner_across = swap(inner, "col", 2)

    picking = [
        pltpu.VMEM((rows * count, 2 * mine, width), BF16),
        pltpu.VMEM((count, 2 * mine, fan_in * width), BF16),
    ]
    total = [pltpu.VMEM((rows * count, mine, width), F32)]

    lower = [None] * (levels - 1)
    got, gathered = gather_row(forward[2])
    early, late = early[:2] + near(early[2]), late[:2] + near(late[2])
    lower[2] = [join(early, 0, cuts[0]), join(late, 0, entries - cuts[0])]
    solved = [None] * levels
    solved[top], *terms = call(
        functools.partial(top_kernel, spans[0]), [block] + [quarter] * 4,
        [SMEM] + [VMEM] * 6 + [VMEM] * len(lower[2]),
        scratch=picking + [pltpu.VMEM((count, mine, width), F32)] + total,
    )(slots[2], *gathered, sides[top], inverse[top], *lower[2])
    outer = pack(flat, [(at0 + cuts[2], entries - cuts[2])], solved[top])
    outer_across = swap(outer, "col", 2)

    got, returned = scatter_row(terms)
    inner = near(inner) + near(after(inner_across, *got))
    lower[1] = [join(late, entries - cuts[0], cuts[1]), join(inner, 0, entries - cuts[1])]
    solved[2], *terms = call(
        functools.partial(backward_kernel, spans[1]), [block] + [quarter] * 4, [SMEM] + [VMEM] * 6, scratch=total,
    )(slots[1], *returned, forward[2], inverse[2], *lower[1])

    got, returned = scatter_row(terms)
    outer = near(outer) + near(after(outer_across, *got))
    lower[0] = [join(inner, entries - cuts[1], cuts[2]), join(outer, 0, entries - cuts[2])]
    solved[1], *terms = call(
        functools.partial(backward_kernel, spans[2]), [block] + [quarter] * 4, [SMEM] + [VMEM] * 6, scratch=total,
    )(slots[0], *returned, forward[1], inverse[1], *lower[0])

    def spread(parts):
        return [parts[0]] + [swap(parts[mask], "col", mask) for mask in range(1, cols)]

    got, returned = scatter_row(terms)
    upper = call(
        functools.partial(cut_kernel, top), [like(top, mine, count * share)] * cols,
        [SMEM] + [VMEM] * (top + len(got)),
        scratch=[pltpu.VMEM((cols, top, mine, count * share), F32)],
    )(col, *solved[1:], *got)
    ahead = call(ahead_kernel, block, [VMEM] * 3)(returned[0], sides[0], inverse[0])
    lowest = call(
        last_kernel, [like(1, mine, count * share)] * cols, [SMEM] + [VMEM] * 3,
        scratch=[
            pltpu.VMEM((count, mine, width), F32),
            pltpu.VMEM((cols, 1, mine, count * share), F32),
        ],
    )(col, returned[1], ahead, inverse[0])
    upper = call(
        upper_kernel, like(top, count, share, columns), [SMEM] + [VMEM] * cols,
        scratch=[pltpu.VMEM((top, columns, count * share), F32)],
    )(col, *spread(upper))
    return pl.pallas_call(
        out_kernel,
        out_shape=like(levels, count, share, columns),
        in_specs=[SMEM] + [VMEM] * (cols + 1),
        out_specs=HBM,
        scratch_shapes=[
            pltpu.VMEM((1, columns, count * share), F32),
            pltpu.VMEM((1, count, share, columns), F32),
            pltpu.SemaphoreType.DMA((2,)),
        ],
        compiler_params=pltpu.CompilerParams(vmem_limit_bytes=24 * 1024 * 1024),
        cost_estimate=TINY,
    )(col, *spread(lowest), upper)


def solution(mesh):
    return jax.shard_map(
        on_device,
        mesh=mesh,
        in_specs=(
            P(None, "row", None, None),
            P(None, "row", "col", None),
            P(None, "row", None, "col", None),
            P(),
        ),
        out_specs=P(None, "row", "col", None),
        check_vma=False,
    )
```

```python
import functools

import jax
import jax.numpy as jnp
from jax import lax
from jax.experimental import pallas as pl
from jax.experimental.pallas import tpu as pltpu
from jax.sharding import PartitionSpec as P

F32 = jnp.float32
BF16 = jnp.bfloat16
EXACT = lax.Precision.HIGHEST
VMEM = pl.BlockSpec(memory_space=pltpu.VMEM)
SMEM = pl.BlockSpec(memory_space=pltpu.SMEM)
ANY = pl.BlockSpec(memory_space=pl.ANY)
HBM = pl.BlockSpec(memory_space=pltpu.HBM)
CUTS = (0.625, 0.25, 0.375)
TINY = pl.CostEstimate(flops=1, bytes_accessed=1, transcendentals=0)


def nn(a, b):
    return lax.dot_general(a, b, (((1,), (0,)), ((), ())), precision=EXACT, preferred_element_type=F32)


def half(a, b, contract):
    return lax.dot_general(a, b, ((contract[:1], contract[1:]), ((), ())), preferred_element_type=F32)


def split(value):
    high = value.astype(BF16)
    return high, (value - high.astype(F32)).astype(BF16)


def times(value, pair):
    rows, width = value.shape[0], pair.shape[1] // 2
    both = half(jnp.concatenate(split(value), axis=0), pair, (1, 0))
    both = both[:, :width] + both[:, width:]
    return both[:rows] + both[rows:]


def times_turned(value, pair):
    rows = value.shape[0]
    high, low = split(value)
    wide = jnp.concatenate([jnp.concatenate([high, high], axis=1), jnp.concatenate([low, low], axis=1)], axis=0)
    both = half(wide, pair, (1, 1))
    return both[:rows] + both[rows:]


def call(body, out_shape, in_specs, scratch=(), limit=24):
    return pl.pallas_call(
        body,
        out_shape=out_shape,
        in_specs=in_specs,
        out_specs=jax.tree.map(lambda _: VMEM, out_shape),
        scratch_shapes=list(scratch),
        compiler_params=pltpu.CompilerParams(vmem_limit_bytes=limit * 1024 * 1024),
        cost_estimate=TINY,
    )


def swap(value, axis, mask):
    size = lax.axis_size(axis)
    return lax.ppermute(value, axis, [(i, i ^ mask) for i in range(size)])


def far_masks(size):
    masks, mask = [], size // 2
    while mask >= 4:
        masks.append(mask)
        mask //= 2
    return masks


def slot_of(mask, size):
    place = (mask & 3) * (size // 4)
    for step, far in enumerate(far_masks(size)):
        place = place + jnp.where((mask & far) != 0, 1 << step, 0)
    return place


def gather_row(own):
    held, got = own, own
    for mask in far_masks(lax.axis_size("row")):
        got = swap(held, "row", mask)
        held = jnp.concatenate([held, got], axis=0)
    return got, [held] + [swap(held, "row", mask) for mask in (1, 2, 3)]


def scatter_row(parts):
    total = parts[0]
    got = [swap(part, "row", mask) for mask, part in zip((1, 2, 3), parts[1:])]
    total = total + got[0] + got[1] + got[2]
    other = None
    for mask in reversed(far_masks(lax.axis_size("row"))):
        if other is not None:
            total = total + other
        keep, send = jnp.split(total, 2, axis=0)
        total, other = keep, swap(send, "row", mask)
    return got, (total, other)


def first_kernel(start, inverse_ref, sides_ref, lower_ref, out_ref, early_ref, inverse, sides, sems):
    copies = [
        pltpu.make_async_copy(inverse_ref.at[0], inverse, sems.at[0]),
        pltpu.make_async_copy(sides_ref.at[0], sides, sems.at[1]),
        pltpu.make_async_copy(lower_ref.at[pl.ds(start, early_ref.shape[0])], early_ref, sems.at[2]),
    ]
    for copy in copies:
        copy.start()
    for copy in copies[:2]:
        copy.wait()
    for j in range(out_ref.shape[0]):
        out_ref[j] = nn(inverse[j], sides[j])
    copies[2].wait()


def join_kernel(place, some, col_ref, *refs):
    parts, out_ref = refs[:-1], refs[-1]
    _, share, width = parts[0].shape
    for mask, part in enumerate(parts):
        offset = pl.multiple_of((col_ref[0] ^ mask) * share, share)
        for d in range(some):
            high, low = split(part[place + d])
            out_ref[pl.ds(d * width + offset, share), :width] = high
            out_ref[pl.ds(d * width + offset, share), width:] = low


def join_inverse_kernel(col_ref, *refs):
    parts, (out_ref, token_ref) = refs[:-2], refs[-2:]
    token_ref[...] = jnp.zeros_like(token_ref)
    share, width = parts[0].shape[1:]
    for mask, part in enumerate(parts):
        offset = pl.multiple_of((col_ref[0] ^ mask) * share, share)
        for i in range(part.shape[0]):
            high, low = split(part[i])
            out_ref[i, pl.ds(offset, share), :width] = high
            out_ref[i, pl.ds(offset, share), width:] = low


def stand_kernel(level, col_ref, lower_ref, all_sides_ref, after_ref, out_ref, sides_ref, own, sides, whole, sems):
    count, fan_in, share, width = own.shape
    copies = [
        pltpu.make_async_copy(all_sides_ref, sides, sems.at[0]),
        pltpu.make_async_copy(lower_ref.at[level], own, sems.at[1]),
    ]
    for copy in copies:
        copy.start()
    copies[0].wait()
    start = pl.multiple_of(col_ref[0] * sides_ref.shape[1], sides_ref.shape[1])
    for i in range(sides_ref.shape[0]):
        whole[i % 2] = sides[i // count, i % count].T
        sides_ref[i] = whole[i % 2, pl.ds(start, sides_ref.shape[1]), :]
    copies[1].wait()
    for j in range(count):
        high, low = split(own[j].reshape(fan_in * share, width).T)
        out_ref[j, :width] = high
        out_ref[j, width:] = low


def fold_kernel(lower_ref, own_inverse_ref, sides_ref, inverse_ref, out_ref, base_ref, own, own_inverse, sides, sems):
    count, fan_in, share, width = own.shape
    copies = [
        pltpu.make_async_copy(lower_ref.at[0], own, sems.at[0]),
        pltpu.make_async_copy(own_inverse_ref.at[1], own_inverse, sems.at[1]),
        pltpu.make_async_copy(sides_ref.at[1], sides, sems.at[2]),
    ]
    for copy in copies:
        copy.start()
    for copy in copies:
        copy.wait()
    for j in range(count):
        high, low = split(times_turned(own[j].reshape(fan_in * share, width), inverse_ref[j]).T)
        out_ref[j, :width] = high
        out_ref[j, width:] = low
        base_ref[j] = nn(own_inverse[j], sides[j])


def partial_kernel(turn, col_ref, slot_ref, x0, x1, x2, x3, lower_ref, *refs):
    outs, (blocks, picked, sums) = refs[-6:-3], refs[-3:]
    count = lower_ref.shape[0]
    fan_in = slot_ref.shape[0] // count
    each, share, columns = x0.shape
    width = lower_ref.shape[1] // 2
    for q, x in enumerate((x0, x1, x2, x3)):
        for i in range(each):
            high, low = split(x[i])
            blocks[q * each + i, :, :columns] = high
            blocks[q * each + i, :, columns:] = low
    for j in range(count):
        for d in range(fan_in):
            picked[j, d * share:(d + 1) * share, :] = blocks[slot_ref[j * fan_in + d]]
    for j in range(count):
        both = half(lower_ref[j], picked[j], (1, 0))
        both = both[:width] + both[width:]
        both = both[:, :columns] + both[:, columns:]
        sums[j] = both.T if turn else both
    each, piece, _ = outs[0].shape
    if turn:
        sums[count] = refs[0][...].reshape(count * share, columns).T
    for place, mask in enumerate((0, 2, 1, 3)):
        start = pl.multiple_of((col_ref[0] ^ mask) * piece, piece)
        out = outs[place] if place < 2 else outs[2].at[pl.ds((place - 2) * each, each)]
        for j in range(each):
            out[j] = sums[j, pl.ds(start, piece), :]


def solve_kernel(col_ref, u0, u1, u2, sides_ref, inverse_ref, out_ref, lower_ref, parts):
    count = out_ref.shape[0]
    share = u0.shape[2] // count
    for j in range(count):
        out_ref[j] = times_turned(sides_ref[j] - ((u0[j] + u1[j]) + u2[j]), inverse_ref[j])
    parts[0], parts[1], parts[2], parts[3] = u0[count], u1[count], u2[count], u2[count + 1]
    for c in range(parts.shape[0]):
        part = parts[col_ref[0] ^ c]
        for j in range(count):
            lower_ref[j, :, c * share:(c + 1) * share] = part[:, j * share:(j + 1) * share]


def runs_of(spans, lower, j, fan_in):
    width = lower[0].shape[1] // 2
    for (start, end), ref in zip(spans, lower):
        low, high = max(start, j * fan_in), min(end, (j + 1) * fan_in)
        if low < high:
            yield low - j * fan_in, high - j * fan_in, ref[(low - start) * width:(high - start) * width, :]


def forward_levels(spans, slot_ref, xs, sides_ref, inverse_ref, lower, out_ref, blocks, picked):
    count, columns, width = out_ref.shape
    fan_in = slot_ref.shape[0] // count
    each = xs[0].shape[0]
    for q, x in enumerate(xs):
        for i in range(each):
            high, low = split(x[i])
            blocks[q * each + i, :columns] = high
            blocks[q * each + i, columns:] = low
    for j in range(count):
        for d in range(fan_in):
            picked[j, :, d * width:(d + 1) * width] = blocks[slot_ref[j * fan_in + d]]
    rest = []
    for j in range(count):
        value = sides_ref[j]
        for low, high, rows in runs_of(spans, lower, j, fan_in):
            both = half(picked[j, :, low * width:high * width], rows, (1, 0))
            both = both[:, :width] + both[:, width:]
            value = value - (both[:columns] + both[columns:])
        rest.append(value)
    for j in range(count):
        out_ref[j] = times_turned(rest[j], inverse_ref[j])


def backward_terms(spans, slot_ref, solved, lower, outs, total):
    count, _, width = solved.shape
    fan_in = slot_ref.shape[0] // count
    total[...] = jnp.zeros_like(total)
    for j in range(count):
        for low, high, rows in runs_of(spans, lower, j, fan_in):
            terms = times_turned(solved[j], rows)
            for d in range(low, high):
                slot = slot_ref[j * fan_in + d]
                total[slot] = total[slot] + terms[:, (d - low) * width:(d - low + 1) * width]
    each = outs[0].shape[0]
    for q, out in enumerate(outs):
        out[...] = total[q * each:(q + 1) * each]


def top_kernel(spans, slot_ref, x0, x1, x2, x3, sides_ref, inverse_ref, *refs):
    chunks = len(spans)
    lower, outs = refs[:chunks], refs[chunks + 1:chunks + 5]
    sol_ref, (blocks, picked, solved, total) = refs[chunks], refs[chunks + 5:]
    forward_levels(spans, slot_ref, (x0, x1, x2, x3), sides_ref, inverse_ref, lower, solved, blocks, picked)
    for j in range(sol_ref.shape[0]):
        sol_ref[j] = times(solved[j], inverse_ref[j])
    backward_terms(spans, slot_ref, sol_ref, lower, outs, total)


def backward_kernel(spans, slot_ref, ret0, ret1, forward_ref, inverse_ref, *refs):
    lower, (sol_ref, *outs, total) = refs[:len(spans)], refs[-6:]
    for j in range(sol_ref.shape[0]):
        sol_ref[j] = times(forward_ref[j] - (ret0[j] + ret1[j]), inverse_ref[j])
    backward_terms(spans, slot_ref, sol_ref, lower, outs, total)


def cut(col_ref, sources, outs, packed):
    share = sources[0].shape[2] // len(outs)
    for level, source in enumerate(sources):
        for c in range(len(outs)):
            packed[c, level] = jnp.concatenate(
                [source[j, :, c * share:(c + 1) * share] for j in range(source.shape[0])], axis=1
            )
    for mask, out in enumerate(outs):
        out[...] = packed[col_ref[0] ^ mask]


def cut_kernel(some, col_ref, *refs):
    cut(col_ref, refs[:some], refs[-5:-1], refs[-1])


def ahead_kernel(ret_ref, sides_ref, inverse_ref, out_ref):
    for j in range(out_ref.shape[0]):
        out_ref[j] = times(times_turned(sides_ref[j], inverse_ref[j]) - ret_ref[j], inverse_ref[j])


def last_kernel(col_ref, ret_ref, ahead_ref, inverse_ref, *refs):
    outs, (solved, packed) = refs[:-2], refs[-2:]
    for j in range(ahead_ref.shape[0]):
        solved[j] = ahead_ref[j] - times(ret_ref[j], inverse_ref[j])
    cut(col_ref, [solved], outs, packed)


def place(col_ref, parts, whole, outs):
    some, piece, columns = parts[0].shape
    for mask, part in enumerate(parts):
        start = pl.multiple_of((col_ref[0] ^ mask) * piece, piece)
        for level in range(some):
            whole[level, pl.ds(start, piece), :] = part[level]
    for level in range(some):
        outs[level] = whole[level].T.reshape(outs.shape[1:])


def upper_kernel(col_ref, *refs):
    place(col_ref, refs[:4], refs[5], refs[4])


def out_kernel(col_ref, *refs):
    parts, (upper_ref, out_ref, whole, lowest, sems) = refs[:4], refs[4:]
    above = pltpu.make_async_copy(upper_ref, out_ref.at[pl.ds(1, upper_ref.shape[0])], sems.at[0])
    above.start()
    place(col_ref, parts, whole, lowest)
    below = pltpu.make_async_copy(lowest, out_ref.at[pl.ds(0, 1)], sems.at[1])
    below.start()
    above.wait()
    below.wait()


def same_kernel(value_ref, *refs):
    refs[-1][...] = value_ref[...]


def after(value, *others, spec=VMEM):
    return pl.pallas_call(
        same_kernel,
        out_shape=jax.ShapeDtypeStruct(value.shape, value.dtype),
        in_specs=[VMEM] + [spec] * len(others),
        out_specs=VMEM,
        compiler_params=pltpu.CompilerParams(vmem_limit_bytes=8 * 1024 * 1024),
        cost_estimate=TINY,
    )(value, *others)


def pack_kernel(pieces, lower_ref, *refs):
    out_ref, sems = refs[-2:]
    copies, place = [], 0
    for i, (start, size) in enumerate(pieces):
        copies.append(pltpu.make_async_copy(lower_ref.at[pl.ds(start, size)], out_ref.at[pl.ds(place, size)], sems.at[i]))
        place += size
    for copy in copies:
        copy.start()
    for copy in copies:
        copy.wait()


def pack(blocks, pieces, *others):
    total = sum(size for _, size in pieces)
    return pl.pallas_call(
        functools.partial(pack_kernel, pieces),
        out_shape=jax.ShapeDtypeStruct((total,) + blocks.shape[1:], F32),
        in_specs=[HBM] + [VMEM] * len(others),
        out_specs=VMEM,
        scratch_shapes=[pltpu.SemaphoreType.DMA((len(pieces),))],
        compiler_params=pltpu.CompilerParams(vmem_limit_bytes=8 * 1024 * 1024),
        cost_estimate=TINY,
    )(blocks, *others)


def on_device(right_sides, inverse_diag, lower_blocks, depends_on):
    levels, count, width, columns = right_sides.shape
    share = inverse_diag.shape[2]
    fan_in = lower_blocks.shape[2]
    rows, cols = lax.axis_size("row"), lax.axis_size("col")
    my_row, my_col = lax.axis_index("row"), lax.axis_index("col")
    col = my_col.astype(jnp.int32).reshape(1)
    mine = columns // cols
    entries = count * fan_in
    wanted = lax.dynamic_slice_in_dim(depends_on, my_row * count, count, 1).reshape(levels - 1, entries)
    slots = slot_of((wanted // count) ^ my_row, rows) * count + wanted % count
    slots = [slots[i] for i in range(levels - 1)]

    def like(*shape, dtype=F32):
        return jax.ShapeDtypeStruct(shape, dtype)

    block = like(count, mine, width)
    quarter = like(rows // 4 * count, mine, width)

    def join(parts, place, some):
        return call(
            functools.partial(join_kernel, place, some), like(some * width, 2 * width, dtype=BF16), [SMEM] + [VMEM] * cols
        )(col, *parts)

    def near(value):
        return value, swap(value, "col", 1)

    top = levels - 1
    flat = lower_blocks.reshape((levels - 1) * entries, share, width)
    unit = fan_in // 2
    cuts = [int(entries * part) // unit * unit for part in CUTS]
    spans = [((0, cut), (cut, entries)) for cut in cuts]
    at2, at1, at0 = (top - 1) * entries, (top - 2) * entries, (top - 3) * entries
    first, early = call(
        functools.partial(first_kernel, at2), [like(count, share, columns), like(cuts[0], share, width)], [HBM] * 3,
        scratch=[
            pltpu.VMEM((count, share, width), F32),
            pltpu.VMEM((count, width, columns), F32),
            pltpu.SemaphoreType.DMA((3,)),
        ],
        limit=60,
    )(inverse_diag, right_sides, flat)
    early = near(early) + (swap(early, "col", 2),)
    _, gathered = gather_row(first)
    all_inverse = inverse_diag.reshape(levels * count, share, width)
    parts_inverse = (all_inverse, swap(after(all_inverse, first), "col", 1)) + near(swap(all_inverse, "col", 2))

    inverse, token = call(
        join_inverse_kernel, [like(levels * count, width, 2 * width, dtype=BF16), like(8, width)], [SMEM] + [VMEM] * cols
    )(col, *parts_inverse)
    inverse = [inverse[i * count:(i + 1) * count] for i in range(levels)]

    folded, base = call(
        fold_kernel, [like(count, 2 * width, fan_in * share, dtype=BF16), like(count, share, columns)], [HBM] * 3 + [VMEM],
        scratch=[
            pltpu.VMEM(lower_blocks.shape[1:], F32),
            pltpu.VMEM((count, share, width), F32),
            pltpu.VMEM((count, width, columns), F32),
            pltpu.SemaphoreType.DMA((3,)),
        ],
    )(lower_blocks, inverse_diag, right_sides, inverse[1])

    def partial(turn, level, gathered, standing, hold, *others):
        each = count + turn
        kept, passed, sent = call(
            functools.partial(partial_kernel, turn), [like(each, share, columns)] * 2 + [like(2 * each, share, columns)],
            [SMEM] * 2 + [VMEM] * (5 + len(others)),
            scratch=[
                pltpu.VMEM((rows * count, share, 2 * columns), BF16),
                pltpu.VMEM((count, fan_in * share, 2 * columns), BF16),
                pltpu.VMEM((each, width, columns), F32),
            ],
        )(col, slots[level], *gathered, standing, *others)
        beside = swap(sent, "col", 1)
        terms = passed[:count] + beside[each:each + count]
        if turn:
            terms = jnp.concatenate([terms, passed[count:], beside[each + count:]], axis=0)
        return kept, beside[:each], swap(after(terms, hold, spec=VMEM if turn else ANY), "col", 2)

    kept, beside, across = partial(False, 0, gathered, folded, early[2])
    forward_rows = base - ((kept + beside) + across)
    late = pack(flat, [(at2 + cuts[0], entries - cuts[0]), (at1, cuts[1])], across)
    late = near(late) + (swap(late, "col", 2),)
    got, gathered = gather_row(forward_rows)

    forward = [None] * levels
    standing, sides = call(
        functools.partial(stand_kernel, 1),
        [like(count, 2 * width, fan_in * share, dtype=BF16), like(levels * count, mine, width)],
        [SMEM, HBM, HBM, VMEM],
        scratch=[
            pltpu.VMEM(lower_blocks.shape[1:], F32),
            pltpu.VMEM(right_sides.shape, F32),
            pltpu.VMEM((2, columns, width), F32),
            pltpu.SemaphoreType.DMA((2,)),
        ],
    )(col, lower_blocks, right_sides, got)
    sides = [sides[i * count:(i + 1) * count] for i in range(levels)]
    updates = partial(True, 1, gathered, standing, late[2], forward_rows)
    forward[2], forward[1] = call(
        solve_kernel, [block] * 2, [SMEM] + [VMEM] * 5, scratch=[pltpu.VMEM((cols, mine, width), F32)]
    )(col, *updates, sides[2], inverse[2])
    inner = pack(flat, [(at1 + cuts[1], entries - cuts[1]), (at0, cuts[2])], forward[2])
    inner_across = swap(inner, "col", 2)

    picking = [
        pltpu.VMEM((rows * count, 2 * mine, width), BF16),
        pltpu.VMEM((count, 2 * mine, fan_in * width), BF16),
    ]
    total = [pltpu.VMEM((rows * count, mine, width), F32)]

    lower = [None] * (levels - 1)
    got, gathered = gather_row(forward[2])
    early, late = early[:2] + near(early[2]), late[:2] + near(late[2])
    lower[2] = [join(early, 0, cuts[0]), join(late, 0, entries - cuts[0])]
    solved = [None] * levels
    solved[top], *terms = call(
        functools.partial(top_kernel, spans[0]), [block] + [quarter] * 4,
        [SMEM] + [VMEM] * 6 + [VMEM] * len(lower[2]),
        scratch=picking + [pltpu.VMEM((count, mine, width), F32)] + total,
    )(slots[2], *gathered, sides[top], inverse[top], *lower[2])
    outer = pack(flat, [(at0 + cuts[2], entries - cuts[2])], solved[top])
    outer_across = swap(outer, "col", 2)

    got, returned = scatter_row(terms)
    inner = near(inner) + near(after(inner_across, *got))
    lower[1] = [join(late, entries - cuts[0], cuts[1]), join(inner, 0, entries - cuts[1])]
    solved[2], *terms = call(
        functools.partial(backward_kernel, spans[1]), [block] + [quarter] * 4, [SMEM] + [VMEM] * 6, scratch=total,
    )(slots[1], *returned, forward[2], inverse[2], *lower[1])

    got, returned = scatter_row(terms)
    outer = near(outer) + near(after(outer_across, *got))
    lower[0] = [join(inner, entries - cuts[1], cuts[2]), join(outer, 0, entries - cuts[2])]
    solved[1], *terms = call(
        functools.partial(backward_kernel, spans[2]), [block] + [quarter] * 4, [SMEM] + [VMEM] * 6, scratch=total,
    )(slots[0], *returned, forward[1], inverse[1], *lower[0])

    def spread(parts):
        return [parts[0]] + [swap(parts[mask], "col", mask) for mask in range(1, cols)]

    got, returned = scatter_row(terms)
    upper = call(
        functools.partial(cut_kernel, top), [like(top, mine, count * share)] * cols,
        [SMEM] + [VMEM] * (top + len(got)),
        scratch=[pltpu.VMEM((cols, top, mine, count * share), F32)],
    )(col, *solved[1:], *got)
    ahead = call(ahead_kernel, block, [VMEM] * 3)(returned[0], sides[0], inverse[0])
    lowest = call(
        last_kernel, [like(1, mine, count * share)] * cols, [SMEM] + [VMEM] * 3,
        scratch=[
            pltpu.VMEM((count, mine, width), F32),
            pltpu.VMEM((cols, 1, mine, count * share), F32),
        ],
    )(col, returned[1], ahead, inverse[0])
    upper = call(
        upper_kernel, like(top, count, share, columns), [SMEM] + [VMEM] * cols,
        scratch=[pltpu.VMEM((top, columns, count * share), F32)],
    )(col, *spread(upper))
    return pl.pallas_call(
        out_kernel,
        out_shape=like(levels, count, share, columns),
        in_specs=[SMEM] + [VMEM] * (cols + 1),
        out_specs=HBM,
        scratch_shapes=[
            pltpu.VMEM((1, columns, count * share), F32),
            pltpu.VMEM((1, count, share, columns), F32),
            pltpu.SemaphoreType.DMA((2,)),
        ],
        compiler_params=pltpu.CompilerParams(vmem_limit_bytes=24 * 1024 * 1024),
        cost_estimate=TINY,
    )(col, *spread(lowest), upper)


def solution(mesh):
    return jax.shard_map(
        on_device,
        mesh=mesh,
        in_specs=(
            P(None, "row", None, None),
            P(None, "row", "col", None),
            P(None, "row", None, "col", None),
            P(),
        ),
        out_specs=P(None, "row", "col", None),
        check_vma=False,
    )
```
